128 devices in a mesh: seq: 32 (over y, x, core), ch: 4 (over z).
Axes of the slice: x: 4, y: 4, z: 4, core: 2. Of those that a mesh axis runs over, the one named last changes fastest.
Arguments:
- token_ids: int32 [8192], P('seq'), may hold values from 65 to 84, as said below
- embedding: bfloat16 [512, 8192], P(None, 'ch'), may hold values from -1200 to 1200
- norm_gain: float32 [8192], P('ch'), may hold values from 0.5 to 1.5
- conv_weight: float32 [3, 7, 8192], P(None, None, 'ch'), may hold values from -2 to 2
- pole_rates: float32 [16, 8192], P(None, 'ch'), may hold values from 0.001 to 0.105
- residues: float32 [16, 8192], P(None, 'ch'), may hold values from -70 to 70
- skip_gain: float32 [8192], P('ch'), may hold values from -1.5 to 1.5
- cotangent: bfloat16 [8192, 8192], P('seq', 'ch'), may hold values from -6 to 6
Outputs:
- hyena_out: bfloat16 [8192, 8192], P('seq', 'ch')
- grad_normed: bfloat16 [8192, 8192], P('seq', 'ch')
- grad_conv: float32 [3, 7, 8192], P(None, None, 'ch')
- grad_residues: float32 [16, 8192], P(None, 'ch')
- grad_skip: float32 [8192], P('ch')
The draws below stay inside these ranges and needn't reach their ends.
Inputs may be any that keep to these rules, and one draw needn't show every extreme that they name: `token_ids`: every token is the byte code of A, C, G or T.
All inputs are finite; a program needn't handle non-finite values.
Results may differ from the reference program's by a relative error of at most 0.03.
Values may be sent and summed in bfloat16 or wider, within the bound.
No kernel may reach another device: no remote copies, remote signals or barrier semaphores. Data moves between devices by JAX's collectives and lax.ppermute only.
A program may use at most 128 MiB of HBM per device.

```python
import jax
import jax.numpy as jnp
from jax import lax

D = 8192
VOCAB = 512
POLES = 16
TAPS = 7
TOKENS = 8192


def draw_token_ids(key, part):
    picks = jax.random.randint(jax.random.fold_in(key, 11), (TOKENS,), 0, 4)
    return (65 + 2 * (picks >= 1) + 4 * (picks >= 2) + 13 * (picks >= 3)).astype(jnp.int32)


def draw_embedding(key, part):
    base_key = jax.random.fold_in(key, 23)
    key_base, key_rows, key_cols = jax.random.split(base_key, 3)
    position = jnp.arange(D, dtype=jnp.float32) / max(D - 1, 1)
    row_scale = jnp.power(10.0, jax.random.uniform(key_rows, (VOCAB, 1), jnp.float32))
    col_base = jnp.power(10.0, jax.random.uniform(key_cols, (1, D), jnp.float32))
    values = jax.random.truncated_normal(key_base, -4.0, 4.0, (VOCAB, D), jnp.float32)
    col_scale = col_base * jnp.power(3.0, position)[None, :]
    return (values * row_scale * col_scale).astype(jnp.bfloat16)


def cluster_draw(key):
    base_key = jax.random.fold_in(key, 41)
    key_base, key_growth, key_magnitude, key_polarity = jax.random.split(base_key, 4)
    clusters = POLES // 4
    grid_shape = (clusters, D)
    growth = jax.random.uniform(key_growth, grid_shape, jnp.float32, 1.35, 1.6)
    fastest = 0.1049 / (growth * growth * growth)
    spread = jnp.log(fastest / 0.001)
    slowest = 0.001 * jnp.exp(spread * jax.random.uniform(key_base, grid_shape, jnp.float32))
    raised = [jnp.ones_like(growth), growth, growth * growth, growth * growth * growth]
    decay_rates = jnp.stack([slowest * factor for factor in raised], 1).reshape(POLES, D)
    magnitude = jnp.exp(jax.random.uniform(key_magnitude, grid_shape, jnp.float32, -0.693, 0.693))
    polarity = jnp.where(jax.random.uniform(key_polarity, grid_shape, jnp.float32) < 0.5, -1.0, 1.0)
    amplitude = 10.0 * magnitude * polarity * slowest / jnp.sqrt(0.035)
    weights = []
    for member in range(4):
        denominator = jnp.ones_like(growth)
        for partner in range(4):
            if partner != member:
                denominator = denominator * (raised[partner] - raised[member])
        weights.append(-amplitude * raised[member] / denominator)
    residue_table = jnp.stack(weights, 1).reshape(POLES, D)
    return (decay_rates, residue_table)


def draw_pole_rates(key, part):
    return cluster_draw(key)[0].astype(jnp.float32)


def draw_residues(key, part):
    return cluster_draw(key)[1].astype(jnp.float32)


def block_scale(stream_key, extent, cuts, least, top_value):
    level, own = 1.0, jax.random.fold_in(stream_key, 6)
    for dim, shards_of in cuts:
        heights = jnp.exp(jax.random.uniform(jax.random.fold_in(own, dim), (shards_of,), jnp.float32, least / len(cuts), top_value / len(cuts)))
        level = level * jnp.repeat(heights, extent[dim] // shards_of).reshape([-1 if axis == dim else 1 for axis in range(len(extent))])
    return level


def gaussian(key, extent, width, most, cuts=(), held_as=jnp.bfloat16):
    entries = jax.random.normal(key, extent, jnp.float32) * width
    if len(cuts) > 0:
        entries = block_scale(key, extent, cuts, -0.22, 0.18) * entries
    return jnp.clip(entries, min=-most, max=most).astype(held_as)


def setup_inputs(seed: int = 0) -> dict:
    key_of = jax.random.split(jax.random.key(seed), 9)
    token_ids = draw_token_ids(jax.random.fold_in(key_of[8], 71), 0)
    embedding = draw_embedding(jax.random.fold_in(key_of[8], 71), 0)
    norm_gain = jnp.clip(1.0 + 0.1 * jax.random.normal(key_of[2], (D,), jnp.float32), 0.5, 1.5)
    conv_weight = gaussian(key_of[3], (3, TAPS, D), TAPS ** -0.5, 2.0, ((2, 4),), jnp.float32)
    pole_rates = draw_pole_rates(jax.random.fold_in(key_of[8], 71), 0)
    residues = draw_residues(jax.random.fold_in(key_of[8], 71), 0)
    skip_gain = gaussian(key_of[6], (D,), 0.25, 1.5, ((0, 4),), jnp.float32)
    cotangent = gaussian(key_of[7], (TOKENS, D), 1.0, 6.0, ((0, 32), (1, 4)))
    return {"token_ids": token_ids, "embedding": embedding, "norm_gain": norm_gain, "conv_weight": conv_weight, "pole_rates": pole_rates, "residues": residues, "skip_gain": skip_gain, "cotangent": cotangent}


def block_pass(scale_rows, embed_block, upstream, gain_block, weight_block, rate_block, residue_block, skip_block):
    length = embed_block.shape[0]
    block_width = embed_block.shape[1]
    normed = (embed_block.astype(jnp.float32) * scale_rows[:, None] * gain_block[None, :]).astype(jnp.bfloat16)
    normed = lax.optimization_barrier(normed)
    padded = jnp.concatenate([jnp.zeros((TAPS - 1, block_width), jnp.bfloat16), normed], 0).astype(jnp.float32)
    features = []
    for feature in range(3):
        summed = jnp.zeros((length, block_width), jnp.float32)
        for offset in range(TAPS):
            summed = summed + weight_block[feature, offset][None, :] * padded[TAPS - 1 - offset:TAPS - 1 - offset + length]
        features.append(summed)
    features = lax.optimization_barrier(jnp.stack(features).astype(jnp.bfloat16)).astype(jnp.float32)
    query_feat = features[0]
    key_feat = features[1]
    value_feat = features[2]
    mixed_kv = key_feat * value_feat
    grad_long = upstream.astype(jnp.float32) * query_feat
    decay_step = jnp.exp(-rate_block)
    zeros_state = jnp.zeros(rate_block.shape, jnp.float32)

    def forward_step(carried, inputs):
        state_now, residue_acc = carried
        mixed_row, grad_row = inputs
        state_now = decay_step * state_now + mixed_row[None, :]
        long_row = lax.optimization_barrier(jnp.sum(residue_block * state_now, 0)) + skip_block * mixed_row
        return ((state_now, residue_acc + grad_row[None, :] * state_now), long_row)
    (spent_state, grad_res), long_conv = lax.scan(forward_step, (zeros_state, zeros_state), (mixed_kv, grad_long))

    def backward_step(adjoint, grad_row):
        adjoint = decay_step * adjoint + grad_row[None, :]
        return (adjoint, skip_block * grad_row + lax.optimization_barrier(jnp.sum(residue_block * adjoint, 0)))
    spent_adjoint, grad_mixed = lax.scan(backward_step, zeros_state, grad_long, reverse=True)
    hyena_out = (query_feat * long_conv).astype(jnp.bfloat16)
    grad_skip = lax.optimization_barrier(jnp.sum(grad_long * mixed_kv, 0))
    feature_grads = jnp.stack([upstream.astype(jnp.float32) * long_conv, grad_mixed * value_feat, grad_mixed * key_feat]).astype(jnp.bfloat16)
    grads_f32 = lax.optimization_barrier(feature_grads).astype(jnp.float32)
    grad_conv = jnp.stack([jnp.stack([lax.optimization_barrier(jnp.sum(grads_f32[feature] * padded[TAPS - 1 - offset:TAPS - 1 - offset + length], 0)) for offset in range(TAPS)]) for feature in range(3)])
    trailing = jnp.concatenate([grads_f32, jnp.zeros((3, TAPS - 1, block_width), jnp.float32)], 1)
    grad_input = jnp.zeros((length, block_width), jnp.float32)
    for feature in range(3):
        for offset in range(TAPS):
            grad_input = grad_input + weight_block[feature, offset][None, :] * trailing[feature, offset:offset + length]
    return (hyena_out, grad_input.astype(jnp.bfloat16), grad_conv, grad_res, grad_skip)

def reference(token_ids, embedding, norm_gain, conv_weight, pole_rates, residues, skip_gain, cotangent):
    embedded = embedding[token_ids]
    widened = embedded.astype(jnp.float32)
    scale_rows = lax.rsqrt(lax.optimization_barrier(jnp.mean(widened * widened, axis=1)) + 1e-05)
    block_width = min(D, 1024)
    blocks = D // block_width

    def to_blocks(array):
        return jnp.moveaxis(array.reshape(array.shape[:-1] + (blocks, block_width)), -2, 0)

    def from_blocks(array):
        return jnp.moveaxis(array, 0, -2).reshape(array.shape[1:-1] + (D,))

    def one_block(pieces):
        return block_pass(scale_rows, pieces[0], pieces[1], pieces[2], pieces[3], pieces[4], pieces[5], pieces[6])
    results = lax.map(one_block, (to_blocks(embedded), to_blocks(cotangent), to_blocks(norm_gain), to_blocks(conv_weight), to_blocks(pole_rates), to_blocks(residues), to_blocks(skip_gain)))
    return (from_blocks(results[0]), from_blocks(results[1]), from_blocks(results[2]), from_blocks(results[3]), from_blocks(results[4]))
```

```python
import jax
import jax.numpy as jnp
from jax import lax
from jax.experimental import pallas as pl
from jax.experimental.pallas import tpu as pltpu
from jax.sharding import PartitionSpec as P

D = 8192
POLES = 16
TAPS = 7
LETTERS = (65, 67, 71, 84)
SEGS = 8
LANES = 128
f32 = jnp.float32
bf16 = jnp.bfloat16


def shifted(block, axis, distance):
    devices = range(lax.axis_size(axis))
    route = [(i - distance, i) for i in devices if i - distance in devices]
    return lax.ppermute(block, axis, route)


def rows(ref, n):
    return jnp.broadcast_to(ref[n : n + 1, :], (SEGS, LANES))


def states_kernel(
    hot_ref, order_ref, embed_ref, scale_ref, gain_ref, weight_ref, rate_ref, cot_ref,
    feat_ref, cotp_ref, normed_ref, inner_ref, ends_ref, x_ref, g_ref,
):
    steps = x_ref.shape[0]
    length = steps * SEGS
    normed = (embed_ref[...] * scale_ref[...] * gain_ref[...]).astype(bf16).astype(f32)
    normed_ref[...] = normed
    cot = jnp.dot(order_ref[...], cot_ref[...], preferred_element_type=f32)
    cotp_ref[...] = cot.astype(bf16)
    feats = []
    for f in range(3):
        table = jnp.concatenate(
            [weight_ref[f, i : i + 1, :] * normed for i in range(TAPS)]
            + [jnp.zeros((SEGS, LANES), f32)],
            0,
        )
        high = table.astype(bf16)
        low = (table - high.astype(f32)).astype(bf16)
        summed = jnp.dot(
            hot_ref[...], jnp.concatenate([high, low], 0), preferred_element_type=f32
        ).astype(bf16)
        feat_ref[f] = summed
        feats.append(summed.astype(f32))
    x_ref[...] = (feats[1] * feats[2]).reshape(steps, SEGS, LANES)
    g_ref[...] = (cot * feats[0]).reshape(steps, SEGS, LANES)
    seg = lax.broadcasted_iota(jnp.int32, (SEGS, LANES), 0)
    for part in range(2):
        base = part * 8
        rates = [rows(rate_ref, base + n) for n in range(8)]
        decay = [jnp.exp(-p) for p in rates]
        for way in range(2):
            src = g_ref if way else x_ref
            state = [jnp.zeros((SEGS, LANES), f32)] * 8
            for i in range(steps):
                now = src[steps - 1 - i if way else i]
                state = [d * s + now for d, s in zip(decay, state)]
            for n in range(8):
                inc = state[n]
                for hop in (1, 2, 4):
                    factor = jnp.exp(rates[n] * (-float(steps * hop)))
                    if way:
                        factor = jnp.where(seg < SEGS - hop, factor, 0.0)
                        inc = inc + factor * pltpu.roll(inc, SEGS - hop, 0)
                    else:
                        factor = jnp.where(seg >= hop, factor, 0.0)
                        inc = inc + factor * pltpu.roll(inc, hop, 0)
                if way:
                    ends_ref[part, 8 + n : 9 + n, :] = inc[0:1]
                    inner = jnp.where(seg < SEGS - 1, pltpu.roll(inc, SEGS - 1, 0), 0.0)
                else:
                    ends_ref[part, n : n + 1, :] = inc[SEGS - 1 :]
                    inner = jnp.where(seg >= 1, pltpu.roll(inc, 1, 0), 0.0)
                inner_ref[way, base + n] = inner


def carry_kernel(length, got_ref, rate_ref, out_ref):
    devices = got_ref.shape[0]
    decay = jnp.exp(rate_ref[...] * (-float(length)))
    state = jnp.zeros((8, LANES), f32)
    for j in range(devices):
        out_ref[j, 0:8, :] = state
        state = decay * state + got_ref[j, 0:8, :]
    state = jnp.zeros((8, LANES), f32)
    for j in reversed(range(devices)):
        out_ref[j, 8:16, :] = state
        state = decay * state + got_ref[j, 8:16, :]


def main_kernel(
    feat_ref, cotp_ref, inner_ref, enter_ref, rate_ref, residue_ref, skip_ref, hot_t_ref,
    order_t_ref, normed_ref,
    out_ref, grads_ref, first_ref, params_ref, x_ref, g_ref, y_ref, m_ref,
):
    steps = x_ref.shape[0]
    length = steps * SEGS
    key = feat_ref[1].astype(f32)
    value = feat_ref[2].astype(f32)
    mixed = key * value
    glong = cotp_ref[...].astype(f32) * feat_ref[0].astype(f32)
    x_ref[...] = mixed.reshape(steps, SEGS, LANES)
    g_ref[...] = glong.reshape(steps, SEGS, LANES)
    skip = jnp.broadcast_to(skip_ref[...], (SEGS, LANES))
    seg = lax.broadcasted_iota(jnp.int32, (SEGS, LANES), 0).astype(f32)
    total = jnp.zeros((SEGS, LANES), f32)
    residue_grads = []
    for part in range(2):
        base = part * 8
        rates = [rows(rate_ref, base + n) for n in range(8)]
        decay = [jnp.exp(-p) for p in rates]
        residue = [rows(residue_ref, base + n) for n in range(8)]
        for way in range(2):
            state = []
            for n in range(8):
                gap = (SEGS - 1.0 - seg) if way else seg
                spread = jnp.exp(rates[n] * (gap * (-float(steps))))
                entering = jnp.broadcast_to(
                    enter_ref[part, 8 * way + n : 8 * way + n + 1, :], (SEGS, LANES)
                )
                state.append(inner_ref[way, base + n] + spread * entering)
            acc = [jnp.zeros((SEGS, LANES), f32)] * 8
            for k in range(steps):
                i = steps - 1 - k if way else k
                src, dst = (g_ref, m_ref) if way else (x_ref, y_ref)
                now = src[i]
                state = [d * s + now for d, s in zip(decay, state)]
                terms = [r * s for r, s in zip(residue, state)]
                while len(terms) > 1:
                    terms = [a + b for a, b in zip(terms[::2], terms[1::2])]
                dst[i] = terms[0] + (dst[i] if part else skip * now)
                if not way:
                    other = g_ref[i]
                    acc = [a + other * s for a, s in zip(acc, state)]
                    if not part:
                        total = total + other * now
            if not way:
                residue_grads += [jnp.sum(a, 0, keepdims=True) for a in acc]
    long_conv = y_ref[...].reshape(length, LANES)
    grad_mixed = m_ref[...].reshape(length, LANES)
    hyena = (feat_ref[0].astype(f32) * long_conv).astype(bf16)
    out_ref[...] = jnp.dot(order_t_ref[...], hyena, preferred_element_type=f32).astype(bf16)
    grads = [
        (cotp_ref[...].astype(f32) * long_conv).astype(bf16),
        (grad_mixed * feat_ref[2].astype(f32)).astype(bf16),
        (grad_mixed * feat_ref[1].astype(f32)).astype(bf16),
    ]
    pieces = residue_grads
    normed = normed_ref[...]
    for f in range(3):
        grads_ref[f] = grads[f]
        wide = grads[f].astype(f32)
        first_ref[f] = jnp.concatenate(
            [wide[8 * i : 8 * i + 1] for i in range(TAPS - 1)] + [jnp.zeros((2, LANES), f32)], 0
        )
        by_token = jnp.dot(hot_t_ref[...], grads[f], preferred_element_type=f32)
        for i in range(TAPS + 1):
            pieces.append(
                jnp.sum(by_token[8 * i : 8 * i + 8] * normed, 0, keepdims=True)
            )
    pieces.append(jnp.sum(total, 0, keepdims=True))
    pieces.append(jnp.zeros((64 - len(pieces), LANES), f32))
    params_ref[...] = jnp.concatenate(pieces, 0).astype(bf16).reshape(2, 32, LANES)


def sum_kernel(got_ref, out_ref):
    total = got_ref[0].astype(f32)
    for j in range(1, got_ref.shape[0]):
        total = total + got_ref[j].astype(f32)
    total = total.astype(bf16)
    for j in range(got_ref.shape[0]):
        out_ref[j] = total


def spread_kernel(got_ref, conv_ref, residue_ref, skip_ref):
    whole = got_ref[...].reshape(64, LANES).astype(f32)
    residue_ref[...] = whole[0:POLES]
    for f in range(3):
        conv_ref[f] = whole[POLES + 8 * f : POLES + 8 * f + TAPS]
    skip_ref[...] = whole[POLES + 24 : POLES + 25]


def input_kernel(grads_ref, after_ref, weight_ref, order_t_ref, out_ref, wide_ref):
    steps = grads_ref.shape[1] // SEGS
    seg = lax.broadcasted_iota(jnp.int32, (SEGS, LANES), 0)
    for f in range(3):
        wide_ref[f, 0:steps] = grads_ref[f].astype(f32).reshape(steps, SEGS, LANES)
        for i in range(TAPS - 1):
            ahead = pltpu.roll(wide_ref[f, i], SEGS - 1, 0)
            last = jnp.broadcast_to(after_ref[f, i : i + 1, :], (SEGS, LANES))
            wide_ref[f, steps + i] = jnp.where(seg < SEGS - 1, ahead, last)
    summed = jnp.zeros((steps, SEGS, LANES), f32)
    for f in range(3):
        for i in range(TAPS):
            summed = summed + weight_ref[f, i : i + 1, :][None] * wide_ref[f, i : i + steps]
    natural = jnp.dot(
        order_t_ref[...], summed.reshape(steps * SEGS, LANES).astype(bf16),
        preferred_element_type=f32,
    )
    out_ref[...] = natural.astype(bf16)


def whole(*shape):
    return pl.BlockSpec(shape, lambda b: (0,) * len(shape))


def lanes(*shape):
    return pl.BlockSpec(shape + (LANES,), lambda b: (0,) * len(shape) + (b,))


def firsts(*shape):
    return pl.BlockSpec(shape, lambda b: (b,) + (0,) * (len(shape) - 1))


def struct(shape, dtype):
    return jax.ShapeDtypeStruct(shape, dtype)


def params_of():
    return pltpu.CompilerParams(vmem_limit_bytes=48 * 1024 * 1024)


def exchange(block):
    return lax.all_to_all(block, "seq", 0, 0, tiled=True)


def per_device(
    token_ids, embedding, norm_gain, conv_weight, pole_rates, residues, skip_gain, cotangent
):
    length = token_ids.shape[0]
    channels = embedding.shape[1]
    margin = TAPS - 1
    steps = length // SEGS
    blocks = channels // LANES
    devices = lax.axis_size("seq")

    embed = jnp.concatenate(
        [embedding[v : v + 1] for v in LETTERS] + [jnp.zeros((4, channels), bf16)], 0
    ).astype(f32)
    sum_squares = lax.psum(jnp.sum(embed * embed, axis=1), "ch")
    scale = jnp.broadcast_to(lax.rsqrt(sum_squares / D + 1e-05)[:, None], (8, LANES))

    leading = shifted(token_ids[length - margin :], "seq", 1)
    padded = jnp.concatenate([leading, token_ids])
    taps = jnp.stack(
        [
            padded[margin - i : margin - i + length].reshape(SEGS, steps).T.reshape(length)
            for i in range(TAPS)
        ]
        + [jnp.zeros((length,), jnp.int32)]
    )
    letters = jnp.array(LETTERS + (-1, -1, -1, -1), jnp.int32)
    hot_t = (taps[:, None, :] == letters[None, :, None]).astype(bf16).reshape(64, length)
    hot = jnp.concatenate([hot_t, hot_t], 0).T
    place = jnp.arange(length, dtype=jnp.int32)
    source = (place % SEGS) * steps + place // SEGS
    order = (source[:, None] == place[None, :]).astype(bf16)
    order_t = (source[None, :] == place[:, None]).astype(bf16)

    feats, cotp, normed, inner, ends = pl.pallas_call(
        states_kernel,
        grid=(blocks,),
        in_specs=[
            whole(length, 128), whole(length, length), lanes(8), whole(8, LANES), lanes(1),
            lanes(3, TAPS), lanes(POLES), lanes(length),
        ],
        out_specs=[
            lanes(3, length), lanes(length), lanes(8), lanes(2, POLES, SEGS),
            firsts(2, 16, LANES),
        ],
        out_shape=[
            struct((3, length, channels), bf16), struct((length, channels), bf16),
            struct((8, channels), f32), struct((2, POLES, SEGS, channels), f32),
            struct((2 * blocks, 16, LANES), f32),
        ],
        scratch_shapes=[pltpu.VMEM((steps, SEGS, LANES), f32)] * 2,
        compiler_params=params_of(),
        name="states",
    )(hot, order, embed, scale, norm_gain[None], conv_weight, pole_rates, cotangent)

    position = lax.axis_index("seq")
    own_rates = lax.dynamic_slice(
        pole_rates, ((position % 2) * 8, (position // 2) * LANES), (8, LANES)
    )
    carried = pl.pallas_call(
        lambda *refs: carry_kernel(length, *refs),
        out_shape=struct((devices, 16, LANES), f32),
        name="carry",
    )(exchange(ends), own_rates)
    entering = exchange(carried)

    hyena, grads, first, params = pl.pallas_call(
        main_kernel,
        grid=(blocks,),
        in_specs=[
            lanes(3, length), lanes(length), lanes(2, POLES, SEGS), firsts(2, 16, LANES),
            lanes(POLES), lanes(POLES), lanes(1), whole(64, length), whole(length, length),
            lanes(8),
        ],
        out_specs=[
            lanes(length), lanes(3, length), lanes(3, 8), firsts(2, 32, LANES),
        ],
        out_shape=[
            struct((length, channels), bf16), struct((3, length, channels), bf16),
            struct((3, 8, channels), f32), struct((2 * blocks, 32, LANES), bf16),
        ],
        scratch_shapes=[pltpu.VMEM((steps, SEGS, LANES), f32)] * 4,
        compiler_params=params_of(),
        name="main",
    )(feats, cotp, inner, entering, pole_rates, residues, skip_gain[None], hot_t, order_t, normed)

    after = shifted(first.astype(bf16), "seq", -1).astype(f32)
    grad_input = pl.pallas_call(
        input_kernel,
        grid=(blocks,),
        in_specs=[lanes(3, length), lanes(3, 8), lanes(3, TAPS), whole(length, length)],
        out_specs=lanes(length),
        out_shape=struct((length, channels), bf16),
        scratch_shapes=[pltpu.VMEM((3, steps + 8, SEGS, LANES), f32)],
        compiler_params=params_of(),
        name="input_grad",
    )(grads, after, conv_weight, order_t)

    summed = pl.pallas_call(
        sum_kernel,
        out_shape=struct((devices, 32, LANES), bf16),
        name="sum",
    )(exchange(params))
    conv_total, residue_total, skip_total = pl.pallas_call(
        spread_kernel,
        grid=(blocks,),
        in_specs=[firsts(2, 32, LANES)],
        out_specs=[lanes(3, TAPS), lanes(POLES), lanes(1)],
        out_shape=[
            struct((3, TAPS, channels), f32), struct((POLES, channels), f32),
            struct((1, channels), f32),
        ],
        name="spread",
    )(exchange(summed))
    return hyena, grad_input, conv_total, residue_total, skip_total[0]


def solution(mesh):
    in_specs = (
        P("seq"),
        P(None, "ch"),
        P("ch"),
        P(None, None, "ch"),
        P(None, "ch"),
        P(None, "ch"),
        P("ch"),
        P("seq", "ch"),
    )
    out_specs = (P("seq", "ch"), P("seq", "ch"), P(None, None, "ch"), P(None, "ch"), P("ch"))
    return jax.shard_map(
        per_device, mesh=mesh, in_specs=in_specs, out_specs=out_specs, check_vma=False
    )
```

```python
import jax
import jax.numpy as jnp
from jax import lax
from jax.experimental import pallas as pl
from jax.experimental.pallas import tpu as pltpu
from jax.sharding import PartitionSpec as P

D = 8192
POLES = 16
TAPS = 7
LETTERS = (65, 67, 71, 84)
FIRST_ROW = 64
SEGS = 8
LANES = 128
HALVES = 4
WIDTH = HALVES * LANES
PARAM_ROWS = 48
f32 = jnp.float32
bf16 = jnp.bfloat16


def rows(ref, n, h):
    return jnp.broadcast_to(ref[n : n + 1, part_of(h)], (SEGS, LANES))


def part_of(h):
    return slice(h * LANES, (h + 1) * LANES)


def tree(terms):
    while len(terms) > 1:
        odd = terms[len(terms) // 2 * 2 :]
        terms = [a + b for a, b in zip(terms[::2], terms[1::2])] + odd
    return terms[0]


def embed_kernel(table_ref, embed_ref, squares_ref):
    wide = table_ref[...].astype(f32)
    picked = [wide[v - FIRST_ROW : v - FIRST_ROW + 1] for v in LETTERS]
    embed = jnp.concatenate(picked + [jnp.zeros((4, wide.shape[1]), f32)], 0)
    embed_ref[...] = embed
    summed = jnp.sum(embed * embed, axis=1, keepdims=True)
    squares_ref[...] = jnp.broadcast_to(summed, squares_ref.shape)


def hot_kernel(tokens_ref, hot_ref, hot_t_ref, order_ref, order_t_ref):
    length = order_ref.shape[0]
    steps = length // SEGS
    margin = TAPS - 1
    letter = lax.broadcasted_iota(jnp.int32, (8, length), 0)
    value = jnp.full((8, length), -1, jnp.int32)
    for n, v in enumerate(LETTERS):
        value = jnp.where(letter == n, v, value)
    tokens = tokens_ref[...]
    pieces = []
    for i in range(TAPS):
        seen = jnp.broadcast_to(tokens[:, margin - i : margin - i + length], (8, length))
        pieces.append(jnp.where(seen == value, 1.0, 0.0))
    pieces.append(jnp.zeros((8, length), f32))
    natural = jnp.concatenate(pieces, 0).astype(bf16)
    row = lax.broadcasted_iota(jnp.int32, (length, length), 0)
    col = lax.broadcasted_iota(jnp.int32, (length, length), 1)
    order = jnp.where((row % SEGS) * steps + row // SEGS == col, 1.0, 0.0).astype(bf16)
    order_t = jnp.where((col % SEGS) * steps + col // SEGS == row, 1.0, 0.0).astype(bf16)
    order_ref[...] = order
    order_t_ref[...] = order_t
    hot_t_ref[...] = jnp.dot(natural, order_t, preferred_element_type=f32).astype(bf16)
    double = jnp.concatenate([natural, natural], 0)
    hot_ref[...] = lax.dot_general(
        order, double, (((1,), (1,)), ((), ())), preferred_element_type=f32
    ).astype(bf16)


def states_kernel(
    hot_ref, order_ref, embed_ref, sum0_ref, sum1_ref, sum2_ref, sum3_ref, gain_ref,
    weight_ref, rate_ref, cot_ref,
    feat_ref, cotp_ref, normed_ref, inner_ref, ends_ref, x_ref, g_ref,
):
    steps = x_ref.shape[1]
    squares = (sum0_ref[...] + sum1_ref[...]) + (sum2_ref[...] + sum3_ref[...])
    scale = lax.rsqrt(squares / D + 1e-05)
    scale = jnp.concatenate([scale] * HALVES, 1)
    normed = (embed_ref[...] * scale * gain_ref[...]).astype(bf16).astype(f32)
    normed_ref[...] = normed
    cot = jnp.dot(order_ref[...], cot_ref[...], preferred_element_type=f32)
    cotp_ref[...] = cot.astype(bf16)
    feats = []
    for f in range(3):
        table = jnp.concatenate(
            [weight_ref[f, i : i + 1, :] * normed for i in range(TAPS)]
            + [jnp.zeros((SEGS, WIDTH), f32)],
            0,
        )
        high = table.astype(bf16)
        low = (table - high.astype(f32)).astype(bf16)
        summed = jnp.dot(
            hot_ref[...], jnp.concatenate([high, low], 0), preferred_element_type=f32
        ).astype(bf16)
        feat_ref[f] = summed
        feats.append(summed.astype(f32))
    mixed = feats[1] * feats[2]
    glong = cot * feats[0]
    for h in range(HALVES):
        x_ref[h] = mixed[:, part_of(h)].reshape(steps, SEGS, LANES)
        g_ref[h] = glong[:, part_of(h)].reshape(steps, SEGS, LANES)
    seg = lax.broadcasted_iota(jnp.int32, (SEGS, LANES), 0)
    for h in range(HALVES):
        for part in range(2):
            base = part * 8
            rates = [rows(rate_ref, base + n, h) for n in range(8)]
            decay = [jnp.exp(-p) for p in rates]
            fwd = [jnp.zeros((SEGS, LANES), f32)] * 8
            bwd = fwd
            for i in range(steps):
                now = x_ref[h, i]
                fwd = [d * s + now for d, s in zip(decay, fwd)]
                now = g_ref[h, steps - 1 - i]
                bwd = [d * s + now for d, s in zip(decay, bwd)]
            for n in range(8):
                inc, dec = fwd[n], bwd[n]
                for hop in (1, 2, 4):
                    factor = jnp.exp(rates[n] * (-float(steps * hop)))
                    inc = inc + jnp.where(seg >= hop, factor, 0.0) * pltpu.roll(inc, hop, 0)
                    dec = dec + jnp.where(seg < SEGS - hop, factor, 0.0) * pltpu.roll(
                        dec, SEGS - hop, 0
                    )
                ends_ref[2 * h + part, n : n + 1, :] = inc[SEGS - 1 :]
                ends_ref[2 * h + part, 8 + n : 9 + n, :] = dec[0:1]
                inner_ref[0, base + n, :, part_of(h)] = jnp.where(
                    seg >= 1, pltpu.roll(inc, 1, 0), 0.0
                )
                inner_ref[1, base + n, :, part_of(h)] = jnp.where(
                    seg < SEGS - 1, pltpu.roll(dec, SEGS - 1, 0), 0.0
                )


def carry_kernel(length, got_ref, rate_ref, out_ref):
    devices = got_ref.shape[0]
    decay = jnp.exp(rate_ref[...] * (-float(length)))
    state = jnp.zeros((8, LANES), f32)
    adjoint = jnp.zeros((8, LANES), f32)
    for j in range(devices):
        out_ref[j, 0:8, :] = state
        state = decay * state + got_ref[j, 0:8, :]
        k = devices - 1 - j
        out_ref[k, 8:16, :] = adjoint
        adjoint = decay * adjoint + got_ref[k, 8:16, :]


def forward_kernel(
    feat_ref, cotp_ref, inner_ref, rate_ref, residue_ref, skip_ref,
    conv_ref, param_ref, x_ref, g_ref,
):
    steps = x_ref.shape[0]
    for h in range(HALVES):
        at = part_of(h)
        mixed = feat_ref[1, :, at].astype(f32) * feat_ref[2, :, at].astype(f32)
        glong = cotp_ref[:, at].astype(f32) * feat_ref[0, :, at].astype(f32)
        x_ref[...] = mixed.reshape(steps, SEGS, LANES)
        g_ref[...] = glong.reshape(steps, SEGS, LANES)
        skip = jnp.broadcast_to(skip_ref[:, at], (SEGS, LANES))
        total = jnp.zeros((SEGS, LANES), f32)
        pieces = []
        for part in range(2):
            base = part * 8
            decay = [jnp.exp(-rows(rate_ref, base + n, h)) for n in range(8)]
            residue = [rows(residue_ref, base + n, h) for n in range(8)]
            state = [inner_ref[0, base + n, :, at] for n in range(8)]
            acc = [jnp.zeros((SEGS, LANES), f32)] * 8
            for i in range(steps):
                now, other = x_ref[i], g_ref[i]
                state = [d * s + now for d, s in zip(decay, state)]
                summed = tree([r * s for r, s in zip(residue, state)])
                spot = slice(SEGS * i, SEGS * i + SEGS)
                conv_ref[spot, at] = summed + (conv_ref[spot, at] if part else skip * now)
                acc = [a + other * s for a, s in zip(acc, state)]
                if not part:
                    total = total + other * now
            pieces += [jnp.sum(a, 0, keepdims=True) for a in acc]
        pieces.append(jnp.sum(total, 0, keepdims=True))
        pieces.append(jnp.zeros((24 - len(pieces), LANES), f32))
        param_ref[:, at] = jnp.concatenate(pieces, 0)


def backward_kernel(
    feat_ref, cotp_ref, inner_ref, rate_ref, residue_ref, skip_ref, grad_ref, g_ref
):
    steps = g_ref.shape[0]
    for h in range(HALVES):
        at = part_of(h)
        glong = cotp_ref[:, at].astype(f32) * feat_ref[0, :, at].astype(f32)
        g_ref[...] = glong.reshape(steps, SEGS, LANES)
        skip = jnp.broadcast_to(skip_ref[:, at], (SEGS, LANES))
        for part in range(2):
            base = part * 8
            decay = [jnp.exp(-rows(rate_ref, base + n, h)) for n in range(8)]
            residue = [rows(residue_ref, base + n, h) for n in range(8)]
            state = [inner_ref[1, base + n, :, at] for n in range(8)]
            for i in reversed(range(steps)):
                now = g_ref[i]
                state = [d * s + now for d, s in zip(decay, state)]
                summed = tree([r * s for r, s in zip(residue, state)])
                spot = slice(SEGS * i, SEGS * i + SEGS)
                grad_ref[spot, at] = summed + (grad_ref[spot, at] if part else skip * now)


def finish_kernel(
    feat_ref, cotp_ref, conv_ref, mixgrad_ref, local_ref, ends_ref, enter_ref, rate_ref,
    residue_ref, hot_t_ref, normed_ref,
    y_ref, grads_ref, first_ref, params_ref, m_ref,
):
    length = y_ref.shape[0]
    steps = length // SEGS
    seg = lax.broadcasted_iota(jnp.int32, (SEGS, LANES), 0).astype(f32)
    for h in range(HALVES):
        at = part_of(h)
        rates = [rows(rate_ref, n, h) for n in range(POLES)]
        decay = [jnp.exp(-p) for p in rates]
        for way in range(2):
            gap = (SEGS - 1.0 - seg) if way else seg
            wave = []
            for n in range(POLES):
                line = 8 * way + n % 8
                entering = enter_ref[2 * h + n // 8, line : line + 1, :]
                start = entering * residue_ref[n : n + 1, at]
                wave.append(jnp.exp(rates[n] * (gap * (-float(steps)))) * start)
            src, dst = (mixgrad_ref, m_ref) if way else (conv_ref, y_ref)
            for k in range(steps):
                i = steps - 1 - k if way else k
                wave = [d * u for d, u in zip(decay, wave)]
                spot = slice(SEGS * i, SEGS * i + SEGS)
                dst[spot, at] = tree([src[spot, at]] + wave)
        for part in range(2):
            span = slice(8 * part, 8 * part + 8)
            cross = (
                enter_ref[2 * h + part, 0:8, :]
                * ends_ref[2 * h + part, 8:16, :]
                * jnp.exp(-rate_ref[span, at])
            )
            params_ref[span, at] = local_ref[span, at] + cross
    long_conv = y_ref[...]
    grad_mixed = m_ref[...]
    grads = [
        (cotp_ref[...].astype(f32) * long_conv).astype(bf16),
        (grad_mixed * feat_ref[2].astype(f32)).astype(bf16),
        (grad_mixed * feat_ref[1].astype(f32)).astype(bf16),
    ]
    normed = normed_ref[...]
    params_ref[40:48, :] = local_ref[16:24, :]
    heads = []
    for f in range(3):
        grads_ref[f] = grads[f]
        wide = grads[f].astype(f32)
        heads += [wide[8 * i : 8 * i + 1] for i in range(TAPS - 1)] + [jnp.zeros((2, WIDTH), f32)]
        by_token = jnp.dot(hot_t_ref[...], grads[f], preferred_element_type=f32)
        params_ref[16 + 8 * f : 24 + 8 * f, :] = jnp.concatenate(
            [
                jnp.sum(by_token[8 * i : 8 * i + 8] * normed, 0, keepdims=True)
                for i in range(TAPS + 1)
            ],
            0,
        )
    heads.append(jnp.zeros((8, WIDTH), f32))
    first_ref[...] = jnp.concatenate(heads, 0).astype(bf16)


def output_kernel(
    feat_ref, y_ref, grads_ref, after_ref, weight_ref, order_t_ref, *rest
):
    hyena_ref, out_ref, wide_ref, sum_ref = rest[-4:]
    hyena = (feat_ref[0].astype(f32) * y_ref[...]).astype(bf16)
    hyena_ref[...] = jnp.dot(order_t_ref[...], hyena, preferred_element_type=f32).astype(bf16)
    after = after_ref[...].astype(f32)
    steps = grads_ref.shape[1] // SEGS
    seg = lax.broadcasted_iota(jnp.int32, (SEGS, LANES), 0)
    for h in range(HALVES):
        at = part_of(h)
        for f in range(3):
            wide_ref[f, 0:steps] = (
                grads_ref[f, :, at].astype(f32).reshape(steps, SEGS, LANES)
            )
        weight = [
            [jnp.broadcast_to(weight_ref[f, i : i + 1, at], (SEGS, LANES)) for i in range(TAPS)]
            for f in range(3)
        ]
        ahead = [[wide_ref[f, i] for i in range(TAPS - 1)] for f in range(3)]
        for i in range(steps):
            terms = []
            for f in range(3):
                j = i + TAPS - 1
                if j < steps:
                    ahead[f].append(wide_ref[f, j])
                else:
                    j -= steps
                    last = jnp.broadcast_to(after[8 * f + j : 8 * f + j + 1, at], (SEGS, LANES))
                    turned = pltpu.roll(wide_ref[f, j], SEGS - 1, 0)
                    ahead[f].append(jnp.where(seg < SEGS - 1, turned, last))
                terms += [w * a for w, a in zip(weight[f], ahead[f])]
                ahead[f] = ahead[f][1:]
            sum_ref[SEGS * i : SEGS * i + SEGS, at] = tree(terms)
    out_ref[...] = jnp.dot(
        order_t_ref[...], sum_ref[...].astype(bf16), preferred_element_type=f32
    ).astype(bf16)


def spread_kernel(core_ref, mine_ref, other_ref, conv_ref, residue_ref, skip_ref):
    mine = mine_ref[...].astype(f32)
    other = other_ref[...].astype(f32)
    upper = core_ref[0] == 1
    both = jnp.concatenate(
        [jnp.where(upper, other, mine), jnp.where(upper, mine, other)], 1
    )
    residue_ref[...] = both[0:POLES]
    for f in range(3):
        conv_ref[f] = both[POLES + 8 * f : POLES + 8 * f + TAPS]
    skip_ref[...] = both[POLES + 24 : POLES + 25]


def whole(*shape):
    return pl.BlockSpec(shape, lambda b: (0,) * len(shape))


def lanes(*shape):
    return pl.BlockSpec(shape + (WIDTH,), lambda b: (0,) * len(shape) + (b,))


def firsts():
    return pl.BlockSpec((2 * HALVES, 16, LANES), lambda b: (b, 0, 0))


def struct(shape, dtype):
    return jax.ShapeDtypeStruct(shape, dtype)


def roomy():
    return pltpu.CompilerParams(vmem_limit_bytes=60 * 1024 * 1024)


def place(y, x, core):
    return y * 8 + x * 2 + core


def turn(block, dy, dx, dcore):
    route = [
        (place(y, x, c), place((y + dy) % 4, (x + dx) % 4, (c + dcore) % 2))
        for y in range(4)
        for x in range(4)
        for c in range(2)
    ]
    return lax.ppermute(block, "seq", route)


def shifted(block, distance):
    devices = range(lax.axis_size("seq"))
    route = [(i - distance, i) for i in devices if i - distance in devices]
    return lax.ppermute(block, "seq", route)


def added(own, *others):
    total = own.astype(f32)
    for other in others:
        total = total + other.astype(f32)
    return total.astype(bf16)


def exchange(block):
    return lax.all_to_all(block, "seq", 0, 0, tiled=True)


def per_device(
    token_ids, embedding, norm_gain, conv_weight, pole_rates, residues, skip_gain, cotangent
):
    length = token_ids.shape[0]
    channels = embedding.shape[1]
    margin = TAPS - 1
    steps = length // SEGS
    count = channels // WIDTH
    grid = (count,)
    owners = 2 * channels // LANES
    position = lax.axis_index("seq")
    core = position % 2

    embed, squares = pl.pallas_call(
        embed_kernel,
        grid=(1,),
        in_specs=[pl.BlockSpec((32, channels), lambda b: (FIRST_ROW // 32, 0))],
        out_specs=[whole(8, channels), whole(8, LANES)],
        out_shape=[struct((8, channels), f32), struct((8, LANES), f32)],
        compiler_params=roomy(),
        name="embed",
    )(embedding)
    leading = shifted(token_ids[length - margin :], 1)
    sums = [squares] + [
        lax.ppermute(squares, "ch", [(i, (i + k) % 4) for i in range(4)]) for k in (1, 2, 3)
    ]
    tail = jnp.zeros((LANES - margin,), jnp.int32)
    tokens = jnp.concatenate([leading, token_ids, tail])[None]
    hot, hot_t, order, order_t = pl.pallas_call(
        hot_kernel,
        out_shape=[
            struct((length, 128), bf16), struct((64, length), bf16),
            struct((length, length), bf16), struct((length, length), bf16),
        ],
        compiler_params=roomy(),
        name="hot",
    )(tokens)

    feats, cotp, normed, inner, ends = pl.pallas_call(
        states_kernel,
        grid=grid,
        in_specs=[whole(length, 128), whole(length, length), lanes(8)]
        + [whole(8, LANES)] * 4
        + [lanes(1), lanes(3, TAPS), lanes(POLES), lanes(length)],
        out_specs=[
            lanes(3, length), lanes(length), lanes(8), lanes(2, POLES, SEGS), firsts(),
        ],
        out_shape=[
            struct((3, length, channels), bf16), struct((length, channels), bf16),
            struct((8, channels), f32), struct((2, POLES, SEGS, channels), f32),
            struct((owners, 16, LANES), f32),
        ],
        scratch_shapes=[pltpu.VMEM((HALVES, steps, SEGS, LANES), f32)] * 2,
        compiler_params=roomy(),
        name="states",
    )(hot, order, embed, *sums, norm_gain[None], conv_weight, pole_rates, cotangent)

    own_rates = lax.dynamic_slice(pole_rates, (core * 8, (position // 2) * LANES), (8, LANES))
    gathered = exchange(ends)
    local = [lanes(3, length), lanes(length), lanes(2, POLES, SEGS), lanes(POLES), lanes(POLES),
             lanes(1)]
    conv_local, param_local = pl.pallas_call(
        forward_kernel,
        grid=grid,
        in_specs=local,
        out_specs=[lanes(length), lanes(24)],
        out_shape=[struct((length, channels), f32), struct((24, channels), f32)],
        scratch_shapes=[pltpu.VMEM((steps, SEGS, LANES), f32)] * 2,
        compiler_params=roomy(),
        name="forward",
    )(feats, cotp, inner, pole_rates, residues, skip_gain[None])
    gathered, conv_local = lax.optimization_barrier((gathered, conv_local))
    carried = pl.pallas_call(
        lambda *refs: carry_kernel(length, *refs),
        out_shape=struct((owners, 16, LANES), f32),
        compiler_params=roomy(),
        name="carry",
    )(gathered, own_rates)
    carried, cotp_late = lax.optimization_barrier((carried, cotp))
    entering = exchange(carried)
    mix_local = pl.pallas_call(
        backward_kernel,
        grid=grid,
        in_specs=local,
        out_specs=lanes(length),
        out_shape=struct((length, channels), f32),
        scratch_shapes=[pltpu.VMEM((steps, SEGS, LANES), f32)],
        compiler_params=roomy(),
        name="backward",
    )(feats, cotp_late, inner, pole_rates, residues, skip_gain[None])

    long_conv, grads, first, params = pl.pallas_call(
        finish_kernel,
        grid=grid,
        in_specs=[
            lanes(3, length), lanes(length), lanes(length), lanes(length), lanes(24), firsts(),
            firsts(), lanes(POLES), lanes(POLES), whole(64, length), lanes(8),
        ],
        out_specs=[lanes(length), lanes(3, length), lanes(32), lanes(PARAM_ROWS)],
        out_shape=[
            struct((length, channels), f32), struct((3, length, channels), bf16),
            struct((32, channels), bf16), struct((PARAM_ROWS, channels), f32),
        ],
        scratch_shapes=[pltpu.VMEM((length, WIDTH), f32)],
        compiler_params=roomy(),
        name="finish",
    )(
        feats, cotp, conv_local, mix_local, param_local, ends, entering, pole_rates, residues,
        hot_t, normed,
    )

    after = shifted(first, -1)
    half = channels // 2
    kept = lax.dynamic_slice(params, (0, core * half), (PARAM_ROWS, half))
    given = lax.dynamic_slice(params, (0, (1 - core) * half), (PARAM_ROWS, half))
    chip = added(kept, turn(given.astype(bf16), 0, 0, 1))
    near = [turn(chip, 0, k, 0) for k in (1, 2, 3)]
    half_grid = count // 2

    def outputs(start, *previous):
        def spot(*shape):
            return pl.BlockSpec(
                shape + (WIDTH,), lambda b: (0,) * len(shape) + (b + start,)
            )

        anywhere = [pl.BlockSpec(memory_space=pl.ANY)] * len(previous)
        return pl.pallas_call(
            output_kernel,
            grid=(half_grid,),
            in_specs=[
                spot(1, length), spot(length), spot(3, length), spot(32), spot(3, TAPS),
                whole(length, length), *anywhere,
            ],
            out_specs=[spot(length), spot(length)],
            out_shape=[struct((length, channels), bf16)] * 2,
            scratch_shapes=[
                pltpu.VMEM((3, steps, SEGS, LANES), f32), pltpu.VMEM((length, WIDTH), f32),
            ],
            input_output_aliases={6: 0, 7: 1} if previous else {},
            compiler_params=roomy(),
            name="outputs",
        )(feats, long_conv, grads, after, conv_weight, order_t, *previous)

    hyena, grad_input = outputs(0)
    *near, hyena, grad_input = lax.optimization_barrier((*near, hyena, grad_input))
    row = added(chip, *near)
    far = [turn(row, k, 0, 0) for k in (1, 2, 3)]
    row, hyena, grad_input = lax.optimization_barrier((row, hyena, grad_input))
    hyena, grad_input = outputs(half_grid, hyena, grad_input)
    *far, hyena, grad_input = lax.optimization_barrier((*far, hyena, grad_input))
    mine = added(row, *far)
    other = turn(mine, 0, 0, 1)
    vmem = pl.BlockSpec(memory_space=pltpu.VMEM)
    conv_total, residue_total, skip_total = pl.pallas_call(
        spread_kernel,
        in_specs=[pl.BlockSpec(memory_space=pltpu.SMEM), vmem, vmem],
        out_shape=[
            struct((3, TAPS, channels), f32), struct((POLES, channels), f32),
            struct((1, channels), f32),
        ],
        compiler_params=roomy(),
        name="spread",
    )(core[None].astype(jnp.int32), mine, other)
    return hyena, grad_input, conv_total, residue_total, skip_total[0]


def solution(mesh):
    in_specs = (
        P("seq"),
        P(None, "ch"),
        P("ch"),
        P(None, None, "ch"),
        P(None, "ch"),
        P(None, "ch"),
        P("ch"),
        P("seq", "ch"),
    )
    out_specs = (P("seq", "ch"), P("seq", "ch"), P(None, None, "ch"), P(None, "ch"), P("ch"))
    return jax.shard_map(
        per_device, mesh=mesh, in_specs=in_specs, out_specs=out_specs, check_vma=False
    )
```

```python
import jax
import jax.numpy as jnp
from jax import lax
from jax.experimental import pallas as pl
from jax.experimental.pallas import tpu as pltpu
from jax.sharding import PartitionSpec as P

D = 8192
POLES = 16
TAPS = 7
LETTERS = (65, 67, 71, 84)
FIRST_ROW = 64
SEGS = 8
LANES = 128
HALVES = 4
WIDTH = HALVES * LANES
PARAM_ROWS = 48
f32 = jnp.float32
bf16 = jnp.bfloat16


def rows(ref, n, h):
    return jnp.broadcast_to(ref[n : n + 1, part_of(h)], (SEGS, LANES))


def part_of(h):
    if isinstance(h, int):
        return slice(h * LANES, (h + 1) * LANES)
    return pl.ds(pl.multiple_of(h * LANES, LANES), LANES)


def each_part(body):
    def step(h, carry):
        body(h)
        return carry

    lax.fori_loop(0, HALVES, step, 0)


def tree(terms):
    while len(terms) > 1:
        odd = terms[len(terms) // 2 * 2 :]
        terms = [a + b for a, b in zip(terms[::2], terms[1::2])] + odd
    return terms[0]


def embed_kernel(table_ref, embed_ref, squares_ref):
    wide = table_ref[...].astype(f32)
    picked = [wide[v - FIRST_ROW : v - FIRST_ROW + 1] for v in LETTERS]
    embed = jnp.concatenate(picked + [jnp.zeros((4, wide.shape[1]), f32)], 0)
    embed_ref[...] = embed
    summed = jnp.sum(embed * embed, axis=1, keepdims=True)
    squares_ref[...] = jnp.broadcast_to(summed, squares_ref.shape)


def hot_kernel(tokens_ref, hot_ref, hot_t_ref, order_ref, order_t_ref):
    length = order_ref.shape[0]
    steps = length // SEGS
    margin = TAPS - 1
    letter = lax.broadcasted_iota(jnp.int32, (8, length), 0)
    value = jnp.full((8, length), -1, jnp.int32)
    for n, v in enumerate(LETTERS):
        value = jnp.where(letter == n, v, value)
    tokens = tokens_ref[...]
    pieces = []
    for i in range(TAPS):
        seen = jnp.broadcast_to(tokens[:, margin - i : margin - i + length], (8, length))
        pieces.append(jnp.where(seen == value, 1.0, 0.0))
    pieces.append(jnp.zeros((8, length), f32))
    natural = jnp.concatenate(pieces, 0).astype(bf16)
    row = lax.broadcasted_iota(jnp.int32, (length, length), 0)
    col = lax.broadcasted_iota(jnp.int32, (length, length), 1)
    order = jnp.where((row % SEGS) * steps + row // SEGS == col, 1.0, 0.0).astype(bf16)
    order_t = jnp.where((col % SEGS) * steps + col // SEGS == row, 1.0, 0.0).astype(bf16)
    order_ref[...] = order
    order_t_ref[...] = order_t
    hot_t_ref[...] = jnp.dot(natural, order_t, preferred_element_type=f32).astype(bf16)
    double = jnp.concatenate([natural, natural], 0)
    hot_ref[...] = lax.dot_general(
        order, double, (((1,), (1,)), ((), ())), preferred_element_type=f32
    ).astype(bf16)


def states_kernel(
    hot_ref, order_ref, embed_ref, sum0_ref, sum1_ref, sum2_ref, sum3_ref, gain_ref,
    weight_ref, rate_ref, cot_ref,
    feat_ref, cotp_ref, normed_ref, inner_ref, ends_ref, x_ref, g_ref,
):
    steps = x_ref.shape[1]
    squares = (sum0_ref[...] + sum1_ref[...]) + (sum2_ref[...] + sum3_ref[...])
    scale = lax.rsqrt(squares / D + 1e-05)
    scale = jnp.concatenate([scale] * HALVES, 1)
    normed = (embed_ref[...] * scale * gain_ref[...]).astype(bf16).astype(f32)
    normed_ref[...] = normed
    cot = jnp.dot(order_ref[...], cot_ref[...], preferred_element_type=f32)
    cotp_ref[...] = cot.astype(bf16)
    feats = []
    for f in range(3):
        table = jnp.concatenate(
            [weight_ref[f, i : i + 1, :] * normed for i in range(TAPS)]
            + [jnp.zeros((SEGS, WIDTH), f32)],
            0,
        )
        high = table.astype(bf16)
        low = (table - high.astype(f32)).astype(bf16)
        summed = jnp.dot(
            hot_ref[...], jnp.concatenate([high, low], 0), preferred_element_type=f32
        ).astype(bf16)
        feat_ref[f] = summed
        feats.append(summed.astype(f32))
    mixed = feats[1] * feats[2]
    glong = cot * feats[0]
    for h in range(HALVES):
        x_ref[h] = mixed[:, part_of(h)].reshape(steps, SEGS, LANES)
        g_ref[h] = glong[:, part_of(h)].reshape(steps, SEGS, LANES)
    seg = lax.broadcasted_iota(jnp.int32, (SEGS, LANES), 0)

    def scan(h):
        for part in range(2):
            base = part * 8
            rates = [rows(rate_ref, base + n, h) for n in range(8)]
            decay = [jnp.exp(-p) for p in rates]
            fwd = [jnp.zeros((SEGS, LANES), f32)] * 8
            bwd = fwd
            for i in range(steps):
                now = x_ref[h, i]
                fwd = [d * s + now for d, s in zip(decay, fwd)]
                now = g_ref[h, steps - 1 - i]
                bwd = [d * s + now for d, s in zip(decay, bwd)]
            for n in range(8):
                inc, dec = fwd[n], bwd[n]
                for hop in (1, 2, 4):
                    factor = jnp.exp(rates[n] * (-float(steps * hop)))
                    inc = inc + jnp.where(seg >= hop, factor, 0.0) * pltpu.roll(inc, hop, 0)
                    dec = dec + jnp.where(seg < SEGS - hop, factor, 0.0) * pltpu.roll(
                        dec, SEGS - hop, 0
                    )
                ends_ref[0, base + n : base + n + 1, part_of(h)] = inc[SEGS - 1 :]
                line = POLES + base + n
                ends_ref[0, line : line + 1, part_of(h)] = dec[0:1]
                inner_ref[0, base + n, :, part_of(h)] = jnp.where(
                    seg >= 1, pltpu.roll(inc, 1, 0), 0.0
                )
                inner_ref[1, base + n, :, part_of(h)] = jnp.where(
                    seg < SEGS - 1, pltpu.roll(dec, SEGS - 1, 0), 0.0
                )

    each_part(scan)


def decays(rate_ref, core, devices):
    half = rate_ref.shape[1] // 2
    spot = pl.ds(pl.multiple_of(core * half, half), half)
    return jnp.exp(rate_ref[:, spot] * (-float(devices)))


def chip_kernel(
    length, place_ref, own_ref, other_ref, rate_ref, chip_ref, pair_ref, *sent_refs
):
    core = place_ref[0] % 2
    y = place_ref[0] // 8
    decay = decays(rate_ref, core, length)
    own, other = own_ref[core], other_ref[core]
    low, high = jnp.where(core == 0, own, other), jnp.where(core == 0, other, own)
    state = decay * low[:POLES] + high[:POLES]
    adjoint = low[POLES:] + decay * high[POLES:]
    chip_ref[0:POLES] = state
    chip_ref[POLES:] = adjoint
    pair_ref[0:POLES] = low[:POLES]
    pair_ref[POLES:] = high[POLES:]
    for k, sent_ref in enumerate(sent_refs):
        sent_ref[...] = jnp.where(y + k + 1 < 4, state, adjoint)


def column_kernel(length, place_ref, chip_ref, got1_ref, got2_ref, got3_ref, rate_ref, *outs):
    core = place_ref[0] % 2
    x = place_ref[0] // 2 % 4
    y = place_ref[0] // 8
    row = decays(rate_ref, core, 8 * length)
    power = [jnp.ones_like(row), row, row * row]
    before = jnp.zeros_like(row)
    behind = jnp.zeros_like(row)
    for k, got_ref in enumerate((got1_ref, got2_ref, got3_ref)):
        got = got_ref[...]
        lower = y >= k + 1
        before = before + jnp.where(lower, power[k] * got, 0.0)
        behind = behind + jnp.where(lower, 0.0, power[2 - k] * got)
    state = chip_ref[0:POLES] + row * before
    adjoint = chip_ref[POLES:] + row * behind
    outs[0][0:POLES] = before
    outs[0][POLES:] = behind
    for k, sent_ref in enumerate(outs[1:]):
        upward = x + k + 1 < 4
        sent_ref[0:POLES] = jnp.where(upward, state, before)
        sent_ref[POLES:] = jnp.where(upward, behind, adjoint)


def row_kernel(
    length, place_ref, pair_ref, column_ref, got1_ref, got2_ref, got3_ref, rate_ref,
    mine_ref, sent_ref,
):
    core = place_ref[0] % 2
    decay = decays(rate_ref, core, length)
    chip = decay * decay
    power = [jnp.ones_like(chip), chip, chip * chip]
    state = power[2] * chip * column_ref[0:POLES]
    adjoint = power[2] * chip * column_ref[POLES:]
    for k, got_ref in enumerate((got1_ref, got2_ref, got3_ref)):
        state = state + power[k] * got_ref[0:POLES]
        adjoint = adjoint + power[2 - k] * got_ref[POLES:]
    first = core == 0
    next_state = decay * state + pair_ref[0:POLES]
    next_adjoint = decay * adjoint + pair_ref[POLES:]
    mine_ref[0:POLES] = jnp.where(first, state, next_state)
    sent_ref[0:POLES] = jnp.where(first, next_state, state)
    mine_ref[POLES:] = jnp.where(first, next_adjoint, adjoint)
    sent_ref[POLES:] = jnp.where(first, adjoint, next_adjoint)


def main_kernel(
    place_ref, feat_ref, cotp_ref, inner_ref, mine_ref, other_ref, rate_ref, residue_ref,
    skip_ref, hot_t_ref, normed_ref,
    y_ref, grads_ref, first_ref, params_ref, m_ref, x_ref, g_ref, enter_ref, sums_ref,
):
    length = y_ref.shape[0]
    steps = length // SEGS
    blocks = pl.num_programs(0)
    here = pl.program_id(0) // (blocks // 2) == place_ref[0] % 2
    enter_ref[...] = jnp.where(here, mine_ref[...], other_ref[...])
    seg = lax.broadcasted_iota(jnp.int32, (SEGS, LANES), 0).astype(f32)

    def scan(h):
        at = part_of(h)
        mixed = feat_ref[1, :, at].astype(f32) * feat_ref[2, :, at].astype(f32)
        glong = cotp_ref[:, at].astype(f32) * feat_ref[0, :, at].astype(f32)
        x_ref[...] = mixed.reshape(steps, SEGS, LANES)
        g_ref[...] = glong.reshape(steps, SEGS, LANES)
        skip = jnp.broadcast_to(skip_ref[:, at], (SEGS, LANES))
        total = jnp.zeros((SEGS, LANES), f32)
        pieces = []
        for part in range(2):
            base = part * 8
            rates = [rows(rate_ref, base + n, h) for n in range(8)]
            decay = [jnp.exp(-p) for p in rates]
            residue = [rows(residue_ref, base + n, h) for n in range(8)]
            for way in range(2):
                gap = ((SEGS - 1.0 - seg) if way else seg) * (-float(steps))
                src, dst = (g_ref, m_ref) if way else (x_ref, y_ref)
                state = [
                    inner_ref[way, base + n, :, at]
                    + jnp.exp(rates[n] * gap)
                    * enter_ref[POLES * way + base + n : POLES * way + base + n + 1, at]
                    for n in range(8)
                ]
                acc = [jnp.zeros((SEGS, LANES), f32)] * 8
                for k in range(steps):
                    i = steps - 1 - k if way else k
                    now = src[i]
                    state = [d * s + now for d, s in zip(decay, state)]
                    summed = tree([r * s for r, s in zip(residue, state)])
                    spot = slice(SEGS * i, SEGS * i + SEGS)
                    dst[spot, at] = summed + (dst[spot, at] if part else skip * now)
                    if not way:
                        other = g_ref[i]
                        acc = [a + other * s for a, s in zip(acc, state)]
                        if not part:
                            total = total + other * now
                if not way:
                    pieces += [jnp.sum(a, 0, keepdims=True) for a in acc]
        sums_ref[0:POLES, at] = jnp.concatenate(pieces, 0)
        sums_ref[40:48, at] = jnp.concatenate(
            [jnp.sum(total, 0, keepdims=True), jnp.zeros((7, LANES), f32)], 0
        )

    each_part(scan)
    long_conv = y_ref[...]
    grad_mixed = m_ref[...]
    grads = [
        (cotp_ref[...].astype(f32) * long_conv).astype(bf16),
        (grad_mixed * feat_ref[2].astype(f32)).astype(bf16),
        (grad_mixed * feat_ref[1].astype(f32)).astype(bf16),
    ]
    normed = normed_ref[...]
    heads = []
    for f in range(3):
        grads_ref[f] = grads[f]
        wide = grads[f][: 8 * TAPS - 8].astype(f32)
        heads += [wide[8 * i : 8 * i + 1] for i in range(TAPS - 1)] + [jnp.zeros((2, WIDTH), f32)]
        by_token = jnp.dot(hot_t_ref[...], grads[f], preferred_element_type=f32)
        sums_ref[16 + 8 * f : 24 + 8 * f, :] = jnp.concatenate(
            [
                jnp.sum(by_token[8 * i : 8 * i + 8] * normed, 0, keepdims=True)
                for i in range(TAPS + 1)
            ],
            0,
        )
    heads.append(jnp.zeros((8, WIDTH), f32))
    first_ref[...] = jnp.concatenate(heads, 0).astype(bf16)
    params_ref[0] = sums_ref[...].astype(bf16)


def output_kernel(
    feat_ref, y_ref, grads_ref, halo_ref, weight_ref, order_t_ref, *rest
):
    hyena_ref, out_ref, wide_ref, sum_ref, after_ref = rest[-5:]
    hyena = (feat_ref[0].astype(f32) * y_ref[...]).astype(bf16)
    hyena_ref[...] = jnp.dot(order_t_ref[...], hyena, preferred_element_type=f32).astype(bf16)
    after_ref[...] = halo_ref[...].astype(f32)
    steps = grads_ref.shape[1] // SEGS
    seg = lax.broadcasted_iota(jnp.int32, (SEGS, LANES), 0)

    def taps(h):
        at = part_of(h)
        for f in range(3):
            wide_ref[f, 0:steps] = (
                grads_ref[f, :, at].astype(f32).reshape(steps, SEGS, LANES)
            )
        weight = [
            [jnp.broadcast_to(weight_ref[f, i : i + 1, at], (SEGS, LANES)) for i in range(TAPS)]
            for f in range(3)
        ]
        ahead = [[wide_ref[f, i] for i in range(TAPS - 1)] for f in range(3)]
        for i in range(steps):
            terms = []
            for f in range(3):
                j = i + TAPS - 1
                if j < steps:
                    ahead[f].append(wide_ref[f, j])
                else:
                    j -= steps
                    last = rows(after_ref, 8 * f + j, h)
                    turned = pltpu.roll(wide_ref[f, j], SEGS - 1, 0)
                    ahead[f].append(jnp.where(seg < SEGS - 1, turned, last))
                terms += [w * a for w, a in zip(weight[f], ahead[f])]
                ahead[f] = ahead[f][1:]
            sum_ref[SEGS * i : SEGS * i + SEGS, at] = tree(terms)

    each_part(taps)
    out_ref[...] = jnp.dot(
        order_t_ref[...], sum_ref[...].astype(bf16), preferred_element_type=f32
    ).astype(bf16)


def spread_kernel(core_ref, mine_ref, other_ref, conv_ref, residue_ref, skip_ref):
    mine = mine_ref[...].astype(f32)
    other = other_ref[...].astype(f32)
    upper = core_ref[0] == 1
    both = jnp.concatenate(
        [jnp.where(upper, other, mine), jnp.where(upper, mine, other)], 1
    )
    residue_ref[...] = both[0:POLES]
    for f in range(3):
        conv_ref[f] = both[POLES + 8 * f : POLES + 8 * f + TAPS]
    skip_ref[...] = both[POLES + 24 : POLES + 25]


def whole(*shape):
    return pl.BlockSpec(shape, lambda b: (0,) * len(shape))


def lanes(*shape):
    return pl.BlockSpec(shape + (WIDTH,), lambda b: (0,) * len(shape) + (b,))


def struct(shape, dtype):
    return jax.ShapeDtypeStruct(shape, dtype)


def roomy(mib=60):
    return pltpu.CompilerParams(vmem_limit_bytes=mib * 1024 * 1024)


def place(y, x, core):
    return y * 8 + x * 2 + core


def turn(block, dy, dx, dcore):
    route = [
        (place(y, x, c), place((y + dy) % 4, (x + dx) % 4, (c + dcore) % 2))
        for y in range(4)
        for x in range(4)
        for c in range(2)
    ]
    return lax.ppermute(block, "seq", route)


def shifted(block, distance):
    devices = range(lax.axis_size("seq"))
    route = [(i - distance, i) for i in devices if i - distance in devices]
    return lax.ppermute(block, "seq", route)


def added(own, *others):
    total = own.astype(f32)
    for other in others:
        total = total + other.astype(f32)
    return total.astype(bf16)


def per_device(
    token_ids, embedding, norm_gain, conv_weight, pole_rates, residues, skip_gain, cotangent
):
    length = token_ids.shape[0]
    channels = embedding.shape[1]
    margin = TAPS - 1
    steps = length // SEGS
    count = channels // WIDTH
    grid = (count,)
    position = lax.axis_index("seq")
    core = position % 2

    embed, squares = pl.pallas_call(
        embed_kernel,
        grid=(1,),
        in_specs=[pl.BlockSpec((32, channels), lambda b: (FIRST_ROW // 32, 0))],
        out_specs=[whole(8, channels), whole(8, LANES)],
        out_shape=[struct((8, channels), f32), struct((8, LANES), f32)],
        compiler_params=roomy(),
        name="embed",
    )(embedding)
    leading = shifted(token_ids[length - margin :], 1)
    sums = [squares] + [
        lax.ppermute(squares, "ch", [(i, (i + k) % 4) for i in range(4)]) for k in (1, 2, 3)
    ]
    tail = jnp.zeros((LANES - margin,), jnp.int32)
    tokens = jnp.concatenate([leading, token_ids, tail])[None]
    hot, hot_t, order, order_t = pl.pallas_call(
        hot_kernel,
        out_shape=[
            struct((length, 128), bf16), struct((64, length), bf16),
            struct((length, length), bf16), struct((length, length), bf16),
        ],
        compiler_params=roomy(),
        name="hot",
    )(tokens)

    feats, cotp, normed, inner, ends = pl.pallas_call(
        states_kernel,
        grid=grid,
        in_specs=[whole(length, 128), whole(length, length), lanes(8)]
        + [whole(8, LANES)] * 4
        + [lanes(1), lanes(3, TAPS), lanes(POLES), lanes(length)],
        out_specs=[
            lanes(3, length), lanes(length), lanes(8), lanes(2, POLES, SEGS),
            pl.BlockSpec((1, 2 * POLES, WIDTH), lambda b: (b // (count // 2), 0, b % (count // 2))),
        ],
        out_shape=[
            struct((3, length, channels), bf16), struct((length, channels), bf16),
            struct((8, channels), f32), struct((2, POLES, SEGS, channels), f32),
            struct((2, 2 * POLES, channels // 2), f32),
        ],
        scratch_shapes=[pltpu.VMEM((HALVES, steps, SEGS, LANES), f32)] * 2,
        compiler_params=roomy(),
        name="states",
    )(hot, order, embed, *sums, norm_gain[None], conv_weight, pole_rates, cotangent)

    place = position[None].astype(jnp.int32)
    smem = pl.BlockSpec(memory_space=pltpu.SMEM)
    vmem = pl.BlockSpec(memory_space=pltpu.VMEM)
    half = channels // 2
    one, two = struct((POLES, half), f32), struct((2 * POLES, half), f32)

    def small(body, name, out_shape, *args):
        return pl.pallas_call(
            lambda *refs: body(length, *refs),
            in_specs=[smem] + [vmem] * len(args),
            out_specs=[vmem] * len(out_shape),
            out_shape=out_shape,
            compiler_params=pltpu.CompilerParams(vmem_limit_bytes=16 * 1024 * 1024),
            name=name,
        )(place, *args)

    paired = turn(ends, 0, 0, 1)
    chip, pair, *sent = small(
        chip_kernel, "chip", [two, two, one, one, one], ends, paired, pole_rates
    )
    got = [turn(block, k + 1, 0, 0) for k, block in enumerate(sent)]
    column, *sent = small(
        column_kernel, "column", [two, two, two, two], chip, *got, pole_rates
    )
    got = [turn(block, 0, k + 1, 0) for k, block in enumerate(sent)]
    mine, sent = small(
        row_kernel, "row", [two, two], pair, column, *got, pole_rates
    )
    other = turn(sent, 0, 0, 1)

    long_conv, grads, first, params = pl.pallas_call(
        main_kernel,
        grid=grid,
        in_specs=[
            smem, lanes(3, length), lanes(length), lanes(2, POLES, SEGS),
            pl.BlockSpec((2 * POLES, WIDTH), lambda b: (0, b % (count // 2))),
            pl.BlockSpec((2 * POLES, WIDTH), lambda b: (0, b % (count // 2))),
            lanes(POLES), lanes(POLES), lanes(1), whole(64, length), lanes(8),
        ],
        out_specs=[
            lanes(length), lanes(3, length), lanes(32),
            pl.BlockSpec(
                (1, PARAM_ROWS, WIDTH), lambda b: (b // (count // 2), 0, b % (count // 2))
            ),
        ],
        out_shape=[
            struct((length, channels), f32), struct((3, length, channels), bf16),
            struct((32, channels), bf16), struct((2, PARAM_ROWS, half), bf16),
        ],
        scratch_shapes=[pltpu.VMEM((length, WIDTH), f32)]
        + [pltpu.VMEM((steps, SEGS, LANES), f32)] * 2
        + [pltpu.VMEM((2 * POLES, WIDTH), f32), pltpu.VMEM((PARAM_ROWS, WIDTH), f32)],
        compiler_params=roomy(60),
        name="main",
    )(
        place, feats, cotp, inner, mine, other, pole_rates, residues, skip_gain[None], hot_t,
        normed,
    )

    after = shifted(first, -1)
    joined = turn(params, 0, 0, 1)
    chip = added(*[lax.dynamic_index_in_dim(p, core, 0, False) for p in (params, joined)])
    near = [turn(chip, 0, k, 0) for k in (1, 2, 3)]
    half_grid = count // 2

    def outputs(start, *previous):
        def spot(*shape):
            return pl.BlockSpec(
                shape + (WIDTH,), lambda b: (0,) * len(shape) + (b + start,)
            )

        anywhere = [pl.BlockSpec(memory_space=pl.ANY)] * len(previous)
        return pl.pallas_call(
            output_kernel,
            grid=(half_grid,),
            in_specs=[
                spot(1, length), spot(length), spot(3, length), spot(32), spot(3, TAPS),
                whole(length, length), *anywhere,
            ],
            out_specs=[spot(length), spot(length)],
            out_shape=[struct((length, channels), bf16)] * 2,
            scratch_shapes=[
                pltpu.VMEM((3, steps, SEGS, LANES), f32), pltpu.VMEM((length, WIDTH), f32),
                pltpu.VMEM((32, WIDTH), f32),
            ],
            input_output_aliases={6: 0, 7: 1} if previous else {},
            compiler_params=roomy(),
            name="outputs",
        )(feats, long_conv, grads, after, conv_weight, order_t, *previous)

    hyena, grad_input = outputs(0)
    *near, hyena, grad_input = lax.optimization_barrier((*near, hyena, grad_input))
    row = added(chip, *near)
    far = [turn(row, k, 0, 0) for k in (1, 2, 3)]
    row, hyena, grad_input = lax.optimization_barrier((row, hyena, grad_input))
    hyena, grad_input = outputs(half_grid, hyena, grad_input)
    *far, hyena, grad_input = lax.optimization_barrier((*far, hyena, grad_input))
    mine = added(row, *far)
    other = turn(mine, 0, 0, 1)
    conv_total, residue_total, skip_total = pl.pallas_call(
        spread_kernel,
        in_specs=[smem, vmem, vmem],
        out_shape=[
            struct((3, TAPS, channels), f32), struct((POLES, channels), f32),
            struct((1, channels), f32),
        ],
        compiler_params=roomy(16),
        name="spread",
    )(core[None].astype(jnp.int32), mine, other)
    return hyena, grad_input, conv_total, residue_total, skip_total[0]


def solution(mesh):
    in_specs = (
        P("seq"),
        P(None, "ch"),
        P("ch"),
        P(None, None, "ch"),
        P(None, "ch"),
        P(None, "ch"),
        P("ch"),
        P("seq", "ch"),
    )
    out_specs = (P("seq", "ch"), P("seq", "ch"), P(None, None, "ch"), P(None, "ch"), P("ch"))
    return jax.shard_map(
        per_device, mesh=mesh, in_specs=in_specs, out_specs=out_specs, check_vma=False
    )
```

```python
import jax
import jax.numpy as jnp
import numpy as np
from jax import lax
from jax.experimental import pallas as pl
from jax.experimental.pallas import tpu as pltpu
from jax.sharding import PartitionSpec as P

D = 8192
POLES = 16
TAPS = 7
LETTERS = (65, 67, 71, 84)
FIRST_ROW = 64
SEGS = 8
LANES = 128
HALVES = 4
WIDTH = HALVES * LANES
PARAM_ROWS = 48
RUN = 8
f32 = jnp.float32
bf16 = jnp.bfloat16


def rows(ref, n, h):
    return jnp.broadcast_to(ref[n : n + 1, part_of(h)], (SEGS, LANES))


def part_of(h):
    if isinstance(h, int):
        return slice(h * LANES, (h + 1) * LANES)
    return pl.ds(pl.multiple_of(h * LANES, LANES), LANES)


def each_part(body):
    def step(h, carry):
        body(h)
        return carry

    lax.fori_loop(0, HALVES, step, 0)


def tree(terms):
    while len(terms) > 1:
        odd = terms[len(terms) // 2 * 2 :]
        terms = [a + b for a, b in zip(terms[::2], terms[1::2])] + odd
    return terms[0]


def embed_kernel(table_ref, embed_ref, squares_ref):
    wide = table_ref[...].astype(f32)
    picked = [wide[v - FIRST_ROW : v - FIRST_ROW + 1] for v in LETTERS]
    embed = jnp.concatenate(picked + [jnp.zeros((4, wide.shape[1]), f32)], 0)
    embed_ref[...] = embed
    summed = jnp.sum(embed * embed, axis=1, keepdims=True)
    squares_ref[...] = jnp.broadcast_to(summed, squares_ref.shape)


def hot_kernel(previous_ref, tokens_ref, hot_ref, hot_t_ref):
    length = tokens_ref.shape[1]
    steps = length // SEGS
    letter = lax.broadcasted_iota(jnp.int32, (8, length), 0)
    value = jnp.full((8, length), -1, jnp.int32)
    for n, v in enumerate(LETTERS):
        value = jnp.where(letter == n, v, value)
    tokens = jnp.concatenate([previous_ref[...], tokens_ref[...]], 1)
    pieces = []
    for i in range(TAPS):
        seen = jnp.broadcast_to(tokens[:, length - i : 2 * length - i], (8, length))
        pieces.append(jnp.where(seen == value, 1.0, 0.0))
    pieces.append(jnp.zeros((8, length), f32))
    natural = jnp.concatenate(pieces, 0).astype(bf16)
    row = lax.broadcasted_iota(jnp.int32, (length, length), 0)
    col = lax.broadcasted_iota(jnp.int32, (length, length), 1)
    order = jnp.where((row % SEGS) * steps + row // SEGS == col, 1.0, 0.0).astype(bf16)
    hot_t_ref[...] = lax.dot_general(
        natural, order, (((1,), (1,)), ((), ())), preferred_element_type=f32).astype(bf16)
    double = jnp.concatenate([natural, natural], 0)
    hot_ref[...] = lax.dot_general(
        order, double, (((1,), (1,)), ((), ())), preferred_element_type=f32
    ).astype(bf16)


def states_kernel(
    hot_ref, order_ref, embed_ref, sum0_ref, sum1_ref, sum2_ref, sum3_ref, gain_ref,
    weight_ref, rate_ref, cot_ref,
    feat_ref, cotp_ref, normed_ref, inner_ref, runs_ref, ends_ref, x_ref, g_ref,
):
    steps = x_ref.shape[1]
    squares = (sum0_ref[...] + sum1_ref[...]) + (sum2_ref[...] + sum3_ref[...])
    scale = lax.rsqrt(squares / D + 1e-05)
    scale = jnp.concatenate([scale] * HALVES, 1)
    normed = (embed_ref[...] * scale * gain_ref[...]).astype(bf16).astype(f32)
    normed_ref[...] = normed
    cot = jnp.dot(order_ref[...], cot_ref[...], preferred_element_type=f32)
    cotp_ref[...] = cot.astype(bf16)
    feats = []
    for f in range(3):
        table = jnp.concatenate(
            [weight_ref[f, i : i + 1, :] * normed for i in range(TAPS)]
            + [jnp.zeros((SEGS, WIDTH), f32)],
            0,
        )
        high = table.astype(bf16)
        low = (table - high.astype(f32)).astype(bf16)
        summed = jnp.dot(
            hot_ref[...], jnp.concatenate([high, low], 0), preferred_element_type=f32
        ).astype(bf16)
        feat_ref[f] = summed
        feats.append(summed.astype(f32))
    mixed = feats[1] * feats[2]
    glong = cot * feats[0]
    for h in range(HALVES):
        x_ref[h] = mixed[:, part_of(h)].reshape(steps, SEGS, LANES)
        g_ref[h] = glong[:, part_of(h)].reshape(steps, SEGS, LANES)
    seg = lax.broadcasted_iota(jnp.int32, (SEGS, LANES), 0)

    def scan(h):
        for part in range(2):
            base = part * 8
            rates = [rows(rate_ref, base + n, h) for n in range(8)]
            decay = [jnp.exp(-p) for p in rates]
            leap = [jnp.exp(p * (-float(RUN))) for p in rates]
            fwd = [jnp.zeros((SEGS, LANES), f32)] * 8
            bwd = fwd
            runs = steps // RUN
            for c in range(runs):
                ahead = [x_ref[h, RUN * c]] * 8
                back = [g_ref[h, steps - 1 - RUN * c]] * 8
                for i in range(RUN * c + 1, RUN * c + RUN):
                    now = x_ref[h, i]
                    ahead = [d * s + now for d, s in zip(decay, ahead)]
                    now = g_ref[h, steps - 1 - i]
                    back = [d * s + now for d, s in zip(decay, back)]
                for n in range(8):
                    runs_ref[0, c, base + n, :, part_of(h)] = ahead[n]
                    runs_ref[1, runs - 1 - c, base + n, :, part_of(h)] = back[n]
                fwd = [e + d * s for e, d, s in zip(ahead, leap, fwd)]
                bwd = [e + d * s for e, d, s in zip(back, leap, bwd)]
            for n in range(8):
                inc, dec = fwd[n], bwd[n]
                for hop in (1, 2, 4):
                    factor = jnp.exp(rates[n] * (-float(steps * hop)))
                    inc = inc + jnp.where(seg >= hop, factor, 0.0) * pltpu.roll(inc, hop, 0)
                    dec = dec + jnp.where(seg < SEGS - hop, factor, 0.0) * pltpu.roll(
                        dec, SEGS - hop, 0
                    )
                ends_ref[0, base + n : base + n + 1, part_of(h)] = inc[SEGS - 1 :]
                line = POLES + base + n
                ends_ref[0, line : line + 1, part_of(h)] = dec[0:1]
                inner_ref[0, base + n, :, part_of(h)] = jnp.where(
                    seg >= 1, pltpu.roll(inc, 1, 0), 0.0
                )
                inner_ref[1, base + n, :, part_of(h)] = jnp.where(
                    seg < SEGS - 1, pltpu.roll(dec, SEGS - 1, 0), 0.0
                )

    each_part(scan)


def decays(rate_ref, core, devices):
    half = rate_ref.shape[1] // 2
    spot = pl.ds(pl.multiple_of(core * half, half), half)
    return jnp.exp(rate_ref[:, spot] * (-float(devices)))


def chip_kernel(
    length, place_ref, own_ref, other_ref, rate_ref, chip_ref, pair_ref, *sent_refs
):
    core = place_ref[0] % 2
    y = place_ref[0] // 8
    decay = decays(rate_ref, core, length)
    own, other = own_ref[core], other_ref[core]
    low, high = jnp.where(core == 0, own, other), jnp.where(core == 0, other, own)
    state = decay * low[:POLES] + high[:POLES]
    adjoint = low[POLES:] + decay * high[POLES:]
    chip_ref[0:POLES] = state
    chip_ref[POLES:] = adjoint
    pair_ref[0:POLES] = low[:POLES]
    pair_ref[POLES:] = high[POLES:]
    for k, sent_ref in enumerate(sent_refs):
        sent_ref[...] = jnp.where(y + k + 1 < 4, state, adjoint)


def column_kernel(length, place_ref, chip_ref, got1_ref, got2_ref, got3_ref, rate_ref, *outs):
    core = place_ref[0] % 2
    x = place_ref[0] // 2 % 4
    y = place_ref[0] // 8
    row = decays(rate_ref, core, 8 * length)
    power = [jnp.ones_like(row), row, row * row]
    before = jnp.zeros_like(row)
    behind = jnp.zeros_like(row)
    for k, got_ref in enumerate((got1_ref, got2_ref, got3_ref)):
        got = got_ref[...]
        lower = y >= k + 1
        before = before + jnp.where(lower, power[k] * got, 0.0)
        behind = behind + jnp.where(lower, 0.0, power[2 - k] * got)
    state = chip_ref[0:POLES] + row * before
    adjoint = chip_ref[POLES:] + row * behind
    outs[0][0:POLES] = before
    outs[0][POLES:] = behind
    for k, sent_ref in enumerate(outs[1:]):
        upward = x + k + 1 < 4
        sent_ref[0:POLES] = jnp.where(upward, state, before)
        sent_ref[POLES:] = jnp.where(upward, behind, adjoint)


def row_kernel(
    length, place_ref, pair_ref, column_ref, got1_ref, got2_ref, got3_ref, rate_ref,
    mine_ref, sent_ref,
):
    core = place_ref[0] % 2
    decay = decays(rate_ref, core, length)
    chip = decay * decay
    power = [jnp.ones_like(chip), chip, chip * chip]
    state = power[2] * chip * column_ref[0:POLES]
    adjoint = power[2] * chip * column_ref[POLES:]
    for k, got_ref in enumerate((got1_ref, got2_ref, got3_ref)):
        state = state + power[k] * got_ref[0:POLES]
        adjoint = adjoint + power[2 - k] * got_ref[POLES:]
    first = core == 0
    next_state = decay * state + pair_ref[0:POLES]
    next_adjoint = decay * adjoint + pair_ref[POLES:]
    mine_ref[0:POLES] = jnp.where(first, state, next_state)
    sent_ref[0:POLES] = jnp.where(first, next_state, state)
    mine_ref[POLES:] = jnp.where(first, next_adjoint, adjoint)
    sent_ref[POLES:] = jnp.where(first, adjoint, next_adjoint)


def main_kernel(
    place_ref, feat_ref, cotp_ref, inner_ref, runs_ref, mine_ref, other_ref, rate_ref,
    residue_ref, skip_ref, hot_t_ref, normed_ref,
    gated_ref, grads_ref, first_ref, params_ref,
    y_ref, m_ref, x_ref, g_ref, enter_ref, sums_ref, wide_ref, cross_ref,
):
    length = y_ref.shape[0]
    steps = length // SEGS
    runs = steps // RUN
    blocks = pl.num_programs(0)
    here = pl.program_id(0) // (blocks // 2) == place_ref[0] % 2
    enter_ref[...] = jnp.where(here, mine_ref[...], other_ref[...])
    seg = lax.broadcasted_iota(jnp.int32, (SEGS, LANES), 0).astype(f32)

    def scan(h):
        at = part_of(h)
        mixed = feat_ref[1, :, at].astype(f32) * feat_ref[2, :, at].astype(f32)
        glong = cotp_ref[:, at].astype(f32) * feat_ref[0, :, at].astype(f32)
        x_ref[...] = mixed.reshape(steps, SEGS, LANES)
        g_ref[...] = glong.reshape(steps, SEGS, LANES)
        packed = jnp.exp(-rate_ref[:, at])
        weight = residue_ref[:, at]
        taps = []
        for k in range(RUN):
            tap = jnp.sum(weight, 0, keepdims=True)
            taps.append(jnp.broadcast_to(tap if k else tap + skip_ref[:, at], (SEGS, LANES)))
            weight = weight * packed
        for n in range(POLES):
            rate = rows(rate_ref, n, h)
            wide_ref[0, n] = jnp.exp(-rate)
            wide_ref[1, n] = jnp.exp(rate * (-float(RUN)))
            wide_ref[2, n] = rows(residue_ref, n, h)
            for way in range(2):
                gap = ((SEGS - 1.0 - seg) if way else seg) * (-float(steps))
                wide_ref[3 + way, n] = inner_ref[way, n, :, at] + jnp.exp(rate * gap) * rows(
                    enter_ref, POLES * way + n, h
                )
        decay = [wide_ref[0, n] for n in range(POLES)]
        for c in range(runs):
            wave = []
            for n in range(POLES):
                state = wide_ref[3, n]
                wave.append(wide_ref[2, n] * state)
                cross = state * runs_ref[1, c, n, :, at]
                cross_ref[n] = cross_ref[n] + cross if c else cross
                wide_ref[3, n] = runs_ref[0, c, n, :, at] + wide_ref[1, n] * state
            for k in range(RUN):
                i = RUN * c + k
                wave = [d * u for d, u in zip(decay, wave)]
                near = [taps[j] * x_ref[i - j] for j in range(k + 1)]
                y_ref[SEGS * i : SEGS * i + SEGS, at] = tree(wave + near)
        for c in reversed(range(runs)):
            wave = []
            for n in range(POLES):
                state = wide_ref[4, n]
                wave.append(wide_ref[2, n] * state)
                wide_ref[4, n] = runs_ref[1, c, n, :, at] + wide_ref[1, n] * state
            for k in range(RUN):
                i = RUN * c + RUN - 1 - k
                wave = [d * u for d, u in zip(decay, wave)]
                near = [taps[j] * g_ref[i + j] for j in range(k + 1)]
                m_ref[SEGS * i : SEGS * i + SEGS, at] = tree(wave + near)
        lags = [[] for _ in range(RUN)]
        for c in range(runs):
            xs = [x_ref[RUN * c + k] for k in range(RUN)]
            gs = [g_ref[RUN * c + k] for k in range(RUN)]
            for k in range(RUN):
                lags[k].append(tree([gs[j] * xs[j - k] for j in range(k, RUN)]))
            if c:
                lags = [[tree(lag)] for lag in lags]
        lags = [jnp.sum(lag[0], 0, keepdims=True) for lag in lags]
        inside = jnp.zeros((POLES, LANES), f32)
        for lag in reversed(lags):
            inside = inside * packed + lag
        across = jnp.concatenate(
            [jnp.sum(cross_ref[n], 0, keepdims=True) for n in range(POLES)], 0
        )
        sums_ref[0:POLES, at] = inside + packed * across
        sums_ref[40:48, at] = jnp.concatenate([lags[0], jnp.zeros((7, LANES), f32)], 0)

    each_part(scan)
    long_conv = y_ref[...]
    gated_ref[...] = (feat_ref[0].astype(f32) * long_conv).astype(bf16)
    grad_mixed = m_ref[...]
    grads = [
        (cotp_ref[...].astype(f32) * long_conv).astype(bf16),
        (grad_mixed * feat_ref[2].astype(f32)).astype(bf16),
        (grad_mixed * feat_ref[1].astype(f32)).astype(bf16),
    ]
    normed = normed_ref[...]
    heads = []
    for f in range(3):
        grads_ref[f] = grads[f]
        wide = grads[f][: 8 * TAPS - 8].astype(f32)
        heads += [wide[8 * i : 8 * i + 1] for i in range(TAPS - 1)] + [jnp.zeros((2, WIDTH), f32)]
        by_token = jnp.dot(hot_t_ref[...], grads[f], preferred_element_type=f32)
        sums_ref[16 + 8 * f : 24 + 8 * f, :] = jnp.concatenate(
            [
                jnp.sum(by_token[8 * i : 8 * i + 8] * normed, 0, keepdims=True)
                for i in range(TAPS + 1)
            ],
            0,
        )
    heads.append(jnp.zeros((8, WIDTH), f32))
    first_ref[...] = jnp.concatenate(heads, 0).astype(bf16)
    params_ref[0] = sums_ref[...].astype(bf16)


def output_kernel(
    gated_ref, grads_ref, halo_ref, weight_ref, order_t_ref, *rest
):
    hyena_ref, out_ref, wide_ref, sum_ref, after_ref = rest[-5:]
    hyena_ref[...] = jnp.dot(
        order_t_ref[...], gated_ref[...], preferred_element_type=f32
    ).astype(bf16)
    after_ref[...] = halo_ref[...].astype(f32)
    steps = grads_ref.shape[1] // SEGS
    seg = lax.broadcasted_iota(jnp.int32, (SEGS, LANES), 0)

    def taps(h):
        at = part_of(h)
        for f in range(3):
            wide_ref[f, 0:steps] = (
                grads_ref[f, :, at].astype(f32).reshape(steps, SEGS, LANES)
            )
        weight = [
            [jnp.broadcast_to(weight_ref[f, i : i + 1, at], (SEGS, LANES)) for i in range(TAPS)]
            for f in range(3)
        ]
        ahead = [[wide_ref[f, i] for i in range(TAPS - 1)] for f in range(3)]
        for i in range(steps):
            terms = []
            for f in range(3):
                j = i + TAPS - 1
                if j < steps:
                    ahead[f].append(wide_ref[f, j])
                else:
                    j -= steps
                    last = rows(after_ref, 8 * f + j, h)
                    turned = pltpu.roll(wide_ref[f, j], SEGS - 1, 0)
                    ahead[f].append(jnp.where(seg < SEGS - 1, turned, last))
                terms += [w * a for w, a in zip(weight[f], ahead[f])]
                ahead[f] = ahead[f][1:]
            sum_ref[SEGS * i : SEGS * i + SEGS, at] = tree(terms)

    each_part(taps)
    out_ref[...] = jnp.dot(
        order_t_ref[...], sum_ref[...].astype(bf16), preferred_element_type=f32
    ).astype(bf16)


def spread_kernel(core_ref, mine_ref, other_ref, conv_ref, residue_ref, skip_ref):
    mine = mine_ref[...].astype(f32)
    other = other_ref[...].astype(f32)
    upper = core_ref[0] == 1
    both = jnp.concatenate(
        [jnp.where(upper, other, mine), jnp.where(upper, mine, other)], 1
    )
    residue_ref[...] = both[0:POLES]
    for f in range(3):
        conv_ref[f] = both[POLES + 8 * f : POLES + 8 * f + TAPS]
    skip_ref[...] = both[POLES + 24 : POLES + 25]


def whole(*shape):
    return pl.BlockSpec(shape, lambda b: (0,) * len(shape))


def lanes(*shape):
    return pl.BlockSpec(shape + (WIDTH,), lambda b: (0,) * len(shape) + (b,))


def struct(shape, dtype):
    return jax.ShapeDtypeStruct(shape, dtype)


def roomy(mib=60):
    return pltpu.CompilerParams(vmem_limit_bytes=mib * 1024 * 1024)


def place(y, x, core):
    return y * 8 + x * 2 + core


def turn(block, dy, dx, dcore):
    route = [
        (place(y, x, c), place((y + dy) % 4, (x + dx) % 4, (c + dcore) % 2))
        for y in range(4)
        for x in range(4)
        for c in range(2)
    ]
    return lax.ppermute(block, "seq", route)


def shifted(block, distance):
    devices = range(lax.axis_size("seq"))
    route = [(i - distance, i) for i in devices if i - distance in devices]
    return lax.ppermute(block, "seq", route)


def added(own, *others):
    total = own.astype(f32)
    for other in others:
        total = total + other.astype(f32)
    return total.astype(bf16)


def per_device(
    token_ids, embedding, norm_gain, conv_weight, pole_rates, residues, skip_gain, cotangent
):
    length = token_ids.shape[0]
    channels = embedding.shape[1]
    steps = length // SEGS
    count = channels // WIDTH
    grid = (count,)
    position = lax.axis_index("seq")
    core = position % 2

    embed, squares = pl.pallas_call(
        embed_kernel,
        grid=(1,),
        in_specs=[pl.BlockSpec((32, channels), lambda b: (FIRST_ROW // 32, 0))],
        out_specs=[whole(8, channels), whole(8, LANES)],
        out_shape=[struct((8, channels), f32), struct((8, LANES), f32)],
        compiler_params=roomy(),
        name="embed",
    )(embedding)
    tokens = token_ids[None]
    previous = shifted(tokens, 1)
    line = np.arange(length)
    table = ((line % SEGS) * steps + line // SEGS)[:, None] == line[None, :]
    order, order_t = jnp.asarray(table, bf16), jnp.asarray(table.T, bf16)
    sums = [squares] + [
        lax.ppermute(squares, "ch", [(i, (i + k) % 4) for i in range(4)]) for k in (1, 2, 3)
    ]
    hot, hot_t = pl.pallas_call(
        hot_kernel,
        out_shape=[struct((length, 128), bf16), struct((64, length), bf16)],
        compiler_params=roomy(),
        name="hot",
    )(previous, tokens)

    feats, cotp, normed, inner, runs, ends = pl.pallas_call(
        states_kernel,
        grid=grid,
        in_specs=[whole(length, 128), whole(length, length), lanes(8)]
        + [whole(8, LANES)] * 4
        + [lanes(1), lanes(3, TAPS), lanes(POLES), lanes(length)],
        out_specs=[
            lanes(3, length), lanes(length), lanes(8), lanes(2, POLES, SEGS),
            lanes(2, steps // RUN, POLES, SEGS),
            pl.BlockSpec((1, 2 * POLES, WIDTH), lambda b: (b // (count // 2), 0, b % (count // 2))),
        ],
        out_shape=[
            struct((3, length, channels), bf16), struct((length, channels), bf16),
            struct((8, channels), f32), struct((2, POLES, SEGS, channels), f32),
            struct((2, steps // RUN, POLES, SEGS, channels), f32),
            struct((2, 2 * POLES, channels // 2), f32),
        ],
        scratch_shapes=[pltpu.VMEM((HALVES, steps, SEGS, LANES), f32)] * 2,
        compiler_params=roomy(),
        name="states",
    )(hot, order, embed, *sums, norm_gain[None], conv_weight, pole_rates, cotangent)

    place = position[None].astype(jnp.int32)
    smem = pl.BlockSpec(memory_space=pltpu.SMEM)
    vmem = pl.BlockSpec(memory_space=pltpu.VMEM)
    half = channels // 2
    one, two = struct((POLES, half), f32), struct((2 * POLES, half), f32)

    def small(body, name, out_shape, *args):
        return pl.pallas_call(
            lambda *refs: body(length, *refs),
            in_specs=[smem] + [vmem] * len(args),
            out_specs=[vmem] * len(out_shape),
            out_shape=out_shape,
            compiler_params=pltpu.CompilerParams(vmem_limit_bytes=16 * 1024 * 1024),
            name=name,
        )(place, *args)

    paired = turn(ends, 0, 0, 1)
    chip, pair, *sent = small(
        chip_kernel, "chip", [two, two, one, one, one], ends, paired, pole_rates
    )
    got = [turn(block, k + 1, 0, 0) for k, block in enumerate(sent)]
    column, *sent = small(
        column_kernel, "column", [two, two, two, two], chip, *got, pole_rates
    )
    got = [turn(block, 0, k + 1, 0) for k, block in enumerate(sent)]
    mine, sent = small(
        row_kernel, "row", [two, two], pair, column, *got, pole_rates
    )
    other = turn(sent, 0, 0, 1)

    gated, grads, first, params = pl.pallas_call(
        main_kernel,
        grid=grid,
        in_specs=[
            smem, lanes(3, length), lanes(length), lanes(2, POLES, SEGS),
            lanes(2, steps // RUN, POLES, SEGS),
            pl.BlockSpec((2 * POLES, WIDTH), lambda b: (0, b % (count // 2))),
            pl.BlockSpec((2 * POLES, WIDTH), lambda b: (0, b % (count // 2))),
            lanes(POLES), lanes(POLES), lanes(1), whole(64, length), lanes(8),
        ],
        out_specs=[
            lanes(length), lanes(3, length), lanes(32),
            pl.BlockSpec(
                (1, PARAM_ROWS, WIDTH), lambda b: (b // (count // 2), 0, b % (count // 2))
            ),
        ],
        out_shape=[
            struct((length, channels), bf16), struct((3, length, channels), bf16),
            struct((32, channels), bf16), struct((2, PARAM_ROWS, half), bf16),
        ],
        scratch_shapes=[pltpu.VMEM((length, WIDTH), f32)] * 2
        + [pltpu.VMEM((steps, SEGS, LANES), f32)] * 2
        + [pltpu.VMEM((2 * POLES, WIDTH), f32), pltpu.VMEM((PARAM_ROWS, WIDTH), f32)]
        + [pltpu.VMEM((5, POLES, SEGS, LANES), f32), pltpu.VMEM((POLES, SEGS, LANES), f32)],
        compiler_params=roomy(60),
        name="main",
    )(
        place, feats, cotp, inner, runs, mine, other, pole_rates, residues, skip_gain[None], hot_t,
        normed,
    )

    after = shifted(first, -1)
    joined = turn(params, 0, 0, 1)
    chip = added(*[lax.dynamic_index_in_dim(p, core, 0, False) for p in (params, joined)])
    near = [turn(chip, 0, k, 0) for k in (1, 2, 3)]
    half_grid = count // 2

    def outputs(start, *previous):
        def spot(*shape):
            return pl.BlockSpec(
                shape + (WIDTH,), lambda b: (0,) * len(shape) + (b + start,)
            )

        anywhere = [pl.BlockSpec(memory_space=pl.ANY)] * len(previous)
        return pl.pallas_call(
            output_kernel,
            grid=(half_grid,),
            in_specs=[
                spot(length), spot(3, length), spot(32), spot(3, TAPS),
                whole(length, length), *anywhere,
            ],
            out_specs=[spot(length), spot(length)],
            out_shape=[struct((length, channels), bf16)] * 2,
            scratch_shapes=[
                pltpu.VMEM((3, steps, SEGS, LANES), f32), pltpu.VMEM((length, WIDTH), f32),
                pltpu.VMEM((32, WIDTH), f32),
            ],
            input_output_aliases={5: 0, 6: 1} if previous else {},
            compiler_params=roomy(),
            name="outputs",
        )(gated, grads, after, conv_weight, order_t, *previous)

    hyena, grad_input = outputs(0)
    *near, hyena, grad_input = lax.optimization_barrier((*near, hyena, grad_input))
    row = added(chip, *near)
    far = [turn(row, k, 0, 0) for k in (1, 2, 3)]
    row, hyena, grad_input = lax.optimization_barrier((row, hyena, grad_input))
    hyena, grad_input = outputs(half_grid, hyena, grad_input)
    *far, hyena, grad_input = lax.optimization_barrier((*far, hyena, grad_input))
    mine = added(row, *far)
    other = turn(mine, 0, 0, 1)
    conv_total, residue_total, skip_total = pl.pallas_call(
        spread_kernel,
        in_specs=[smem, vmem, vmem],
        out_shape=[
            struct((3, TAPS, channels), f32), struct((POLES, channels), f32),
            struct((1, channels), f32),
        ],
        compiler_params=roomy(16),
        name="spread",
    )(core[None].astype(jnp.int32), mine, other)
    return hyena, grad_input, conv_total, residue_total, skip_total[0]


def solution(mesh):
    in_specs = (
        P("seq"),
        P(None, "ch"),
        P("ch"),
        P(None, None, "ch"),
        P(None, "ch"),
        P(None, "ch"),
        P("ch"),
        P("seq", "ch"),
    )
    out_specs = (P("seq", "ch"), P("seq", "ch"), P(None, None, "ch"), P(None, "ch"), P("ch"))
    return jax.shard_map(
        per_device, mesh=mesh, in_specs=in_specs, out_specs=out_specs, check_vma=False
    )
```

```python
import jax
import jax.numpy as jnp
import numpy as np
from jax import lax
from jax.experimental import pallas as pl
from jax.experimental.pallas import tpu as pltpu
from jax.sharding import PartitionSpec as P

D = 8192
POLES = 16
TAPS = 7
LETTERS = (65, 67, 71, 84)
FIRST_ROW = 64
SEGS = 8
LANES = 128
HALVES = 4
WIDTH = HALVES * LANES
PARAM_ROWS = 48
RUN = 8
SCAN_WIDTH = 2 * LANES
f32 = jnp.float32
bf16 = jnp.bfloat16


def rows(ref, n, h):
    return jnp.broadcast_to(ref[n : n + 1, part_of(h)], (SEGS, LANES))


def part_of(h):
    if isinstance(h, int):
        return slice(h * LANES, (h + 1) * LANES)
    return pl.ds(pl.multiple_of(h * LANES, LANES), LANES)


def each_part(body, parts=HALVES):
    def step(h, carry):
        body(h)
        return carry

    lax.fori_loop(0, parts, step, 0)


def tree(terms):
    while len(terms) > 1:
        odd = terms[len(terms) // 2 * 2 :]
        terms = [a + b for a, b in zip(terms[::2], terms[1::2])] + odd
    return terms[0]


def embed_kernel(table_ref, embed_ref, squares_ref):
    wide = table_ref[...].astype(f32)
    picked = [wide[v - FIRST_ROW : v - FIRST_ROW + 1] for v in LETTERS]
    embed = jnp.concatenate(picked + [jnp.zeros((4, wide.shape[1]), f32)], 0)
    embed_ref[...] = embed
    summed = jnp.sum(embed * embed, axis=1, keepdims=True)
    squares_ref[...] = jnp.broadcast_to(summed, squares_ref.shape)


def hot_kernel(previous_ref, tokens_ref, hot_ref, hot_t_ref):
    length = tokens_ref.shape[1]
    steps = length // SEGS
    letter = lax.broadcasted_iota(jnp.int32, (8, length), 0)
    value = jnp.full((8, length), -1, jnp.int32)
    for n, v in enumerate(LETTERS):
        value = jnp.where(letter == n, v, value)
    tokens = jnp.concatenate([previous_ref[...], tokens_ref[...]], 1)
    pieces = []
    for i in range(TAPS):
        seen = jnp.broadcast_to(tokens[:, length - i : 2 * length - i], (8, length))
        pieces.append(jnp.where(seen == value, 1.0, 0.0))
    pieces.append(jnp.zeros((8, length), f32))
    natural = jnp.concatenate(pieces, 0).astype(bf16)
    row = lax.broadcasted_iota(jnp.int32, (length, length), 0)
    col = lax.broadcasted_iota(jnp.int32, (length, length), 1)
    order = jnp.where((row % SEGS) * steps + row // SEGS == col, 1.0, 0.0).astype(bf16)
    hot_t_ref[...] = lax.dot_general(
        natural, order, (((1,), (1,)), ((), ())), preferred_element_type=f32).astype(bf16)
    double = jnp.concatenate([natural, natural], 0)
    hot_ref[...] = lax.dot_general(
        order, double, (((1,), (1,)), ((), ())), preferred_element_type=f32
    ).astype(bf16)


def states_kernel(
    hot_ref, order_ref, embed_ref, sum0_ref, sum1_ref, sum2_ref, sum3_ref, gain_ref,
    weight_ref, rate_ref, cot_ref,
    feat_ref, cotp_ref, normed_ref, inner_ref, runs_ref, ends_ref, x_ref, g_ref,
):
    steps = x_ref.shape[1]
    squares = (sum0_ref[...] + sum1_ref[...]) + (sum2_ref[...] + sum3_ref[...])
    scale = lax.rsqrt(squares / D + 1e-05)
    scale = jnp.concatenate([scale] * HALVES, 1)
    normed = (embed_ref[...] * scale * gain_ref[...]).astype(bf16).astype(f32)
    normed_ref[...] = normed
    cot = jnp.dot(order_ref[...], cot_ref[...], preferred_element_type=f32)
    cotp_ref[...] = cot.astype(bf16)
    feats = []
    for f in range(3):
        table = jnp.concatenate(
            [weight_ref[f, i : i + 1, :] * normed for i in range(TAPS)]
            + [jnp.zeros((SEGS, WIDTH), f32)],
            0,
        )
        high = table.astype(bf16)
        low = (table - high.astype(f32)).astype(bf16)
        summed = jnp.dot(
            hot_ref[...], jnp.concatenate([high, low], 0), preferred_element_type=f32
        ).astype(bf16)
        feat_ref[f] = summed
        feats.append(summed.astype(f32))
    mixed = feats[1] * feats[2]
    glong = cot * feats[0]
    for h in range(HALVES):
        x_ref[h] = mixed[:, part_of(h)].reshape(steps, SEGS, LANES)
        g_ref[h] = glong[:, part_of(h)].reshape(steps, SEGS, LANES)
    seg = lax.broadcasted_iota(jnp.int32, (SEGS, LANES), 0)

    def scan(h):
        for part in range(2):
            base = part * 8
            rates = [rows(rate_ref, base + n, h) for n in range(8)]
            decay = [jnp.exp(-p) for p in rates]
            leap = [jnp.exp(p * (-float(RUN))) for p in rates]
            fwd = [jnp.zeros((SEGS, LANES), f32)] * 8
            bwd = fwd
            runs = steps // RUN
            for c in range(runs):
                ahead = [x_ref[h, RUN * c]] * 8
                back = [g_ref[h, steps - 1 - RUN * c]] * 8
                for i in range(RUN * c + 1, RUN * c + RUN):
                    now = x_ref[h, i]
                    ahead = [d * s + now for d, s in zip(decay, ahead)]
                    now = g_ref[h, steps - 1 - i]
                    back = [d * s + now for d, s in zip(decay, back)]
                for n in range(8):
                    runs_ref[0, c, base + n, :, part_of(h)] = ahead[n]
                    runs_ref[1, runs - 1 - c, base + n, :, part_of(h)] = back[n]
                fwd = [e + d * s for e, d, s in zip(ahead, leap, fwd)]
                bwd = [e + d * s for e, d, s in zip(back, leap, bwd)]
            for n in range(8):
                inc, dec = fwd[n], bwd[n]
                for hop in (1, 2, 4):
                    factor = jnp.exp(rates[n] * (-float(steps * hop)))
                    inc = inc + jnp.where(seg >= hop, factor, 0.0) * pltpu.roll(inc, hop, 0)
                    dec = dec + jnp.where(seg < SEGS - hop, factor, 0.0) * pltpu.roll(
                        dec, SEGS - hop, 0
                    )
                ends_ref[0, base + n : base + n + 1, part_of(h)] = inc[SEGS - 1 :]
                line = POLES + base + n
                ends_ref[0, line : line + 1, part_of(h)] = dec[0:1]
                inner_ref[0, base + n, :, part_of(h)] = jnp.where(
                    seg >= 1, pltpu.roll(inc, 1, 0), 0.0
                )
                inner_ref[1, base + n, :, part_of(h)] = jnp.where(
                    seg < SEGS - 1, pltpu.roll(dec, SEGS - 1, 0), 0.0
                )

    each_part(scan)


def decays(rate_ref, core, devices):
    half = rate_ref.shape[1] // 2
    spot = pl.ds(pl.multiple_of(core * half, half), half)
    return jnp.exp(rate_ref[:, spot] * (-float(devices)))


def chip_kernel(
    length, place_ref, own_ref, other_ref, rate_ref, chip_ref, pair_ref, *sent_refs
):
    core = place_ref[0] % 2
    y = place_ref[0] // 8
    decay = decays(rate_ref, core, length)
    own, other = own_ref[core], other_ref[core]
    low, high = jnp.where(core == 0, own, other), jnp.where(core == 0, other, own)
    state = decay * low[:POLES] + high[:POLES]
    adjoint = low[POLES:] + decay * high[POLES:]
    chip_ref[0:POLES] = state
    chip_ref[POLES:] = adjoint
    pair_ref[0:POLES] = low[:POLES]
    pair_ref[POLES:] = high[POLES:]
    for k, sent_ref in enumerate(sent_refs):
        sent_ref[...] = jnp.where(y + k + 1 < 4, state, adjoint)


def column_kernel(length, place_ref, chip_ref, got1_ref, got2_ref, got3_ref, rate_ref, *outs):
    core = place_ref[0] % 2
    x = place_ref[0] // 2 % 4
    y = place_ref[0] // 8
    row = decays(rate_ref, core, 8 * length)
    power = [jnp.ones_like(row), row, row * row]
    before = jnp.zeros_like(row)
    behind = jnp.zeros_like(row)
    for k, got_ref in enumerate((got1_ref, got2_ref, got3_ref)):
        got = got_ref[...]
        lower = y >= k + 1
        before = before + jnp.where(lower, power[k] * got, 0.0)
        behind = behind + jnp.where(lower, 0.0, power[2 - k] * got)
    state = chip_ref[0:POLES] + row * before
    adjoint = chip_ref[POLES:] + row * behind
    outs[0][0:POLES] = before
    outs[0][POLES:] = behind
    for k, sent_ref in enumerate(outs[1:]):
        upward = x + k + 1 < 4
        sent_ref[0:POLES] = jnp.where(upward, state, before)
        sent_ref[POLES:] = jnp.where(upward, behind, adjoint)


def row_kernel(
    length, place_ref, pair_ref, column_ref, got1_ref, got2_ref, got3_ref, rate_ref,
    mine_ref, sent_ref,
):
    core = place_ref[0] % 2
    decay = decays(rate_ref, core, length)
    chip = decay * decay
    power = [jnp.ones_like(chip), chip, chip * chip]
    state = power[2] * chip * column_ref[0:POLES]
    adjoint = power[2] * chip * column_ref[POLES:]
    for k, got_ref in enumerate((got1_ref, got2_ref, got3_ref)):
        state = state + power[k] * got_ref[0:POLES]
        adjoint = adjoint + power[2 - k] * got_ref[POLES:]
    first = core == 0
    next_state = decay * state + pair_ref[0:POLES]
    next_adjoint = decay * adjoint + pair_ref[POLES:]
    mine_ref[0:POLES] = jnp.where(first, state, next_state)
    sent_ref[0:POLES] = jnp.where(first, next_state, state)
    mine_ref[POLES:] = jnp.where(first, next_adjoint, adjoint)
    sent_ref[POLES:] = jnp.where(first, adjoint, next_adjoint)


def main_kernel(
    place_ref, feat_ref, cotp_ref, inner_ref, runs_ref, mine_ref, other_ref, rate_ref,
    residue_ref, skip_ref, hot_t_ref, normed_ref,
    gated_ref, grads_ref, first_ref, params_ref,
    y_ref, m_ref, x_ref, g_ref, enter_ref, sums_ref, wide_ref, cross_ref,
):
    length = y_ref.shape[0]
    steps = length // SEGS
    runs = steps // RUN
    blocks = pl.num_programs(0)
    here = pl.program_id(0) // (blocks // 2) == place_ref[0] % 2
    enter_ref[...] = jnp.where(here, mine_ref[...], other_ref[...])
    seg = lax.broadcasted_iota(jnp.int32, (SEGS, LANES), 0).astype(f32)

    def scan(h):
        at = part_of(h)
        mixed = feat_ref[1, :, at].astype(f32) * feat_ref[2, :, at].astype(f32)
        glong = cotp_ref[:, at].astype(f32) * feat_ref[0, :, at].astype(f32)
        x_ref[...] = mixed.reshape(steps, SEGS, LANES)
        g_ref[...] = glong.reshape(steps, SEGS, LANES)
        packed = jnp.exp(-rate_ref[:, at])
        weight = residue_ref[:, at]
        taps = []
        for k in range(RUN):
            tap = jnp.sum(weight, 0, keepdims=True)
            taps.append(jnp.broadcast_to(tap if k else tap + skip_ref[:, at], (SEGS, LANES)))
            weight = weight * packed
        for n in range(POLES):
            rate = rows(rate_ref, n, h)
            wide_ref[0, n] = jnp.exp(-rate)
            wide_ref[1, n] = jnp.exp(rate * (-float(RUN)))
            wide_ref[2, n] = rows(residue_ref, n, h)
            for way in range(2):
                gap = ((SEGS - 1.0 - seg) if way else seg) * (-float(steps))
                wide_ref[3 + way, n] = inner_ref[way, n, :, at] + jnp.exp(rate * gap) * rows(
                    enter_ref, POLES * way + n, h
                )
        decay = [wide_ref[0, n] for n in range(POLES)]
        for c in range(runs):
            wave = []
            for n in range(POLES):
                state = wide_ref[3, n]
                wave.append(wide_ref[2, n] * state)
                cross = state * runs_ref[1, c, n, :, at]
                cross_ref[n] = cross_ref[n] + cross if c else cross
                wide_ref[3, n] = runs_ref[0, c, n, :, at] + wide_ref[1, n] * state
            for k in range(RUN):
                i = RUN * c + k
                wave = [d * u for d, u in zip(decay, wave)]
                near = [taps[j] * x_ref[i - j] for j in range(k + 1)]
                y_ref[SEGS * i : SEGS * i + SEGS, at] = tree(wave + near)
        for c in reversed(range(runs)):
            wave = []
            for n in range(POLES):
                state = wide_ref[4, n]
                wave.append(wide_ref[2, n] * state)
                wide_ref[4, n] = runs_ref[1, c, n, :, at] + wide_ref[1, n] * state
            for k in range(RUN):
                i = RUN * c + RUN - 1 - k
                wave = [d * u for d, u in zip(decay, wave)]
                near = [taps[j] * g_ref[i + j] for j in range(k + 1)]
                m_ref[SEGS * i : SEGS * i + SEGS, at] = tree(wave + near)
        lags = [[] for _ in range(RUN)]
        for c in range(runs):
            xs = [x_ref[RUN * c + k] for k in range(RUN)]
            gs = [g_ref[RUN * c + k] for k in range(RUN)]
            for k in range(RUN):
                lags[k].append(tree([gs[j] * xs[j - k] for j in range(k, RUN)]))
            if c:
                lags = [[tree(lag)] for lag in lags]
        lags = [jnp.sum(lag[0], 0, keepdims=True) for lag in lags]
        inside = jnp.zeros((POLES, LANES), f32)
        for lag in reversed(lags):
            inside = inside * packed + lag
        across = jnp.concatenate(
            [jnp.sum(cross_ref[n], 0, keepdims=True) for n in range(POLES)], 0
        )
        sums_ref[0:POLES, at] = inside + packed * across
        sums_ref[40:48, at] = jnp.concatenate([lags[0], jnp.zeros((7, LANES), f32)], 0)

    each_part(scan, SCAN_WIDTH // LANES)
    long_conv = y_ref[...]
    gated_ref[...] = (feat_ref[0].astype(f32) * long_conv).astype(bf16)
    grad_mixed = m_ref[...]
    grads = [
        (cotp_ref[...].astype(f32) * long_conv).astype(bf16),
        (grad_mixed * feat_ref[2].astype(f32)).astype(bf16),
        (grad_mixed * feat_ref[1].astype(f32)).astype(bf16),
    ]
    normed = normed_ref[...]
    heads = []
    for f in range(3):
        grads_ref[f] = grads[f]
        wide = grads[f][: 8 * TAPS - 8].astype(f32)
        heads += [wide[8 * i : 8 * i + 1] for i in range(TAPS - 1)] + [jnp.zeros((2, SCAN_WIDTH), f32)]
        by_token = jnp.dot(hot_t_ref[...], grads[f], preferred_element_type=f32)
        sums_ref[16 + 8 * f : 24 + 8 * f, :] = jnp.concatenate(
            [
                jnp.sum(by_token[8 * i : 8 * i + 8] * normed, 0, keepdims=True)
                for i in range(TAPS + 1)
            ],
            0,
        )
    heads.append(jnp.zeros((8, SCAN_WIDTH), f32))
    first_ref[...] = jnp.concatenate(heads, 0).astype(bf16)
    params_ref[0] = sums_ref[...].astype(bf16)


def output_kernel(
    gated_ref, grads_ref, halo_ref, weight_ref, order_t_ref, *rest
):
    hyena_ref, out_ref, wide_ref, sum_ref, after_ref = rest[-5:]
    hyena_ref[...] = jnp.dot(
        order_t_ref[...], gated_ref[...], preferred_element_type=f32
    ).astype(bf16)
    after_ref[...] = halo_ref[...].astype(f32)
    steps = grads_ref.shape[1] // SEGS
    seg = lax.broadcasted_iota(jnp.int32, (SEGS, LANES), 0)

    def taps(h):
        at = part_of(h)
        for f in range(3):
            wide_ref[f, 0:steps] = (
                grads_ref[f, :, at].astype(f32).reshape(steps, SEGS, LANES)
            )
        weight = [
            [jnp.broadcast_to(weight_ref[f, i : i + 1, at], (SEGS, LANES)) for i in range(TAPS)]
            for f in range(3)
        ]
        ahead = [[wide_ref[f, i] for i in range(TAPS - 1)] for f in range(3)]
        for i in range(steps):
            terms = []
            for f in range(3):
                j = i + TAPS - 1
                if j < steps:
                    ahead[f].append(wide_ref[f, j])
                else:
                    j -= steps
                    last = rows(after_ref, 8 * f + j, h)
                    turned = pltpu.roll(wide_ref[f, j], SEGS - 1, 0)
                    ahead[f].append(jnp.where(seg < SEGS - 1, turned, last))
                terms += [w * a for w, a in zip(weight[f], ahead[f])]
                ahead[f] = ahead[f][1:]
            sum_ref[SEGS * i : SEGS * i + SEGS, at] = tree(terms)

    each_part(taps)
    out_ref[...] = jnp.dot(
        order_t_ref[...], sum_ref[...].astype(bf16), preferred_element_type=f32
    ).astype(bf16)


def spread_kernel(core_ref, mine_ref, other_ref, conv_ref, residue_ref, skip_ref):
    mine = mine_ref[...].astype(f32)
    other = other_ref[...].astype(f32)
    upper = core_ref[0] == 1
    both = jnp.concatenate(
        [jnp.where(upper, other, mine), jnp.where(upper, mine, other)], 1
    )
    residue_ref[...] = both[0:POLES]
    for f in range(3):
        conv_ref[f] = both[POLES + 8 * f : POLES + 8 * f + TAPS]
    skip_ref[...] = both[POLES + 24 : POLES + 25]


def whole(*shape):
    return pl.BlockSpec(shape, lambda b: (0,) * len(shape))


def lanes(*shape):
    return pl.BlockSpec(shape + (WIDTH,), lambda b: (0,) * len(shape) + (b,))


def struct(shape, dtype):
    return jax.ShapeDtypeStruct(shape, dtype)


def roomy(mib=60):
    return pltpu.CompilerParams(vmem_limit_bytes=mib * 1024 * 1024)


def place(y, x, core):
    return y * 8 + x * 2 + core


def turn(block, dy, dx, dcore):
    route = [
        (place(y, x, c), place((y + dy) % 4, (x + dx) % 4, (c + dcore) % 2))
        for y in range(4)
        for x in range(4)
        for c in range(2)
    ]
    return lax.ppermute(block, "seq", route)


def shifted(block, distance):
    devices = range(lax.axis_size("seq"))
    route = [(i - distance, i) for i in devices if i - distance in devices]
    return lax.ppermute(block, "seq", route)


def added(own, *others):
    total = own.astype(f32)
    for other in others:
        total = total + other.astype(f32)
    return total.astype(bf16)


def per_device(
    token_ids, embedding, norm_gain, conv_weight, pole_rates, residues, skip_gain, cotangent
):
    length = token_ids.shape[0]
    channels = embedding.shape[1]
    steps = length // SEGS
    count = channels // WIDTH
    grid = (count,)
    position = lax.axis_index("seq")
    core = position % 2

    embed, squares = pl.pallas_call(
        embed_kernel,
        grid=(1,),
        in_specs=[pl.BlockSpec((32, channels), lambda b: (FIRST_ROW // 32, 0))],
        out_specs=[whole(8, channels), whole(8, LANES)],
        out_shape=[struct((8, channels), f32), struct((8, LANES), f32)],
        compiler_params=roomy(),
        name="embed",
    )(embedding)
    tokens = token_ids[None]
    previous = shifted(tokens, 1)
    line = np.arange(length)
    table = ((line % SEGS) * steps + line // SEGS)[:, None] == line[None, :]
    order, order_t = jnp.asarray(table, bf16), jnp.asarray(table.T, bf16)
    sums = [squares] + [
        lax.ppermute(squares, "ch", [(i, (i + k) % 4) for i in range(4)]) for k in (1, 2, 3)
    ]
    hot, hot_t = pl.pallas_call(
        hot_kernel,
        out_shape=[struct((length, 128), bf16), struct((64, length), bf16)],
        compiler_params=roomy(),
        name="hot",
    )(previous, tokens)

    feats, cotp, normed, inner, runs, ends = pl.pallas_call(
        states_kernel,
        grid=grid,
        in_specs=[whole(length, 128), whole(length, length), lanes(8)]
        + [whole(8, LANES)] * 4
        + [lanes(1), lanes(3, TAPS), lanes(POLES), lanes(length)],
        out_specs=[
            lanes(3, length), lanes(length), lanes(8), lanes(2, POLES, SEGS),
            lanes(2, steps // RUN, POLES, SEGS),
            pl.BlockSpec((1, 2 * POLES, WIDTH), lambda b: (b // (count // 2), 0, b % (count // 2))),
        ],
        out_shape=[
            struct((3, length, channels), bf16), struct((length, channels), bf16),
            struct((8, channels), f32), struct((2, POLES, SEGS, channels), f32),
            struct((2, steps // RUN, POLES, SEGS, channels), f32),
            struct((2, 2 * POLES, channels // 2), f32),
        ],
        scratch_shapes=[pltpu.VMEM((HALVES, steps, SEGS, LANES), f32)] * 2,
        compiler_params=roomy(),
        name="states",
    )(hot, order, embed, *sums, norm_gain[None], conv_weight, pole_rates, cotangent)

    place = position[None].astype(jnp.int32)
    smem = pl.BlockSpec(memory_space=pltpu.SMEM)
    vmem = pl.BlockSpec(memory_space=pltpu.VMEM)
    half = channels // 2
    one, two = struct((POLES, half), f32), struct((2 * POLES, half), f32)

    def small(body, name, out_shape, *args):
        return pl.pallas_call(
            lambda *refs: body(length, *refs),
            in_specs=[smem] + [vmem] * len(args),
            out_specs=[vmem] * len(out_shape),
            out_shape=out_shape,
            compiler_params=pltpu.CompilerParams(vmem_limit_bytes=16 * 1024 * 1024),
            name=name,
        )(place, *args)

    paired = turn(ends, 0, 0, 1)
    chip, pair, *sent = small(
        chip_kernel, "chip", [two, two, one, one, one], ends, paired, pole_rates
    )
    got = [turn(block, k + 1, 0, 0) for k, block in enumerate(sent)]
    column, *sent = small(
        column_kernel, "column", [two, two, two, two], chip, *got, pole_rates
    )
    got = [turn(block, 0, k + 1, 0) for k, block in enumerate(sent)]
    mine, sent = small(
        row_kernel, "row", [two, two], pair, column, *got, pole_rates
    )
    other = turn(sent, 0, 0, 1)

    span = channels // SCAN_WIDTH // 2

    def slim(*shape):
        return pl.BlockSpec(shape + (SCAN_WIDTH,), lambda b: (0,) * len(shape) + (b,))

    gated, grads, first, params = pl.pallas_call(
        main_kernel,
        grid=(2 * span,),
        in_specs=[
            smem, slim(3, length), slim(length), slim(2, POLES, SEGS),
            slim(2, steps // RUN, POLES, SEGS),
            pl.BlockSpec((2 * POLES, SCAN_WIDTH), lambda b: (0, b % span)),
            pl.BlockSpec((2 * POLES, SCAN_WIDTH), lambda b: (0, b % span)),
            slim(POLES), slim(POLES), slim(1), whole(64, length), slim(8),
        ],
        out_specs=[
            slim(length), slim(3, length), slim(32),
            pl.BlockSpec(
                (1, PARAM_ROWS, SCAN_WIDTH), lambda b: (b // span, 0, b % span)
            ),
        ],
        out_shape=[
            struct((length, channels), bf16), struct((3, length, channels), bf16),
            struct((32, channels), bf16), struct((2, PARAM_ROWS, half), bf16),
        ],
        scratch_shapes=[pltpu.VMEM((length, SCAN_WIDTH), f32)] * 2
        + [pltpu.VMEM((steps, SEGS, LANES), f32)] * 2
        + [pltpu.VMEM((2 * POLES, SCAN_WIDTH), f32), pltpu.VMEM((PARAM_ROWS, SCAN_WIDTH), f32)]
        + [pltpu.VMEM((5, POLES, SEGS, LANES), f32), pltpu.VMEM((POLES, SEGS, LANES), f32)],
        compiler_params=roomy(60),
        name="main",
    )(
        place, feats, cotp, inner, runs, mine, other, pole_rates, residues, skip_gain[None], hot_t,
        normed,
    )

    after = shifted(first, -1)
    joined = turn(params, 0, 0, 1)
    chip = added(*[lax.dynamic_index_in_dim(p, core, 0, False) for p in (params, joined)])
    near = [turn(chip, 0, k, 0) for k in (1, 2, 3)]
    half_grid = count // 2

    def outputs(start, *previous):
        def spot(*shape):
            return pl.BlockSpec(
                shape + (WIDTH,), lambda b: (0,) * len(shape) + (b + start,)
            )

        anywhere = [pl.BlockSpec(memory_space=pl.ANY)] * len(previous)
        return pl.pallas_call(
            output_kernel,
            grid=(half_grid,),
            in_specs=[
                spot(length), spot(3, length), spot(32), spot(3, TAPS),
                whole(length, length), *anywhere,
            ],
            out_specs=[spot(length), spot(length)],
            out_shape=[struct((length, channels), bf16)] * 2,
            scratch_shapes=[
                pltpu.VMEM((3, steps, SEGS, LANES), f32), pltpu.VMEM((length, WIDTH), f32),
                pltpu.VMEM((32, WIDTH), f32),
            ],
            input_output_aliases={5: 0, 6: 1} if previous else {},
            compiler_params=roomy(),
            name="outputs",
        )(gated, grads, after, conv_weight, order_t, *previous)

    hyena, grad_input = outputs(0)
    *near, hyena, grad_input = lax.optimization_barrier((*near, hyena, grad_input))
    row = added(chip, *near)
    far = [turn(row, k, 0, 0) for k in (1, 2, 3)]
    row, hyena, grad_input = lax.optimization_barrier((row, hyena, grad_input))
    hyena, grad_input = outputs(half_grid, hyena, grad_input)
    *far, hyena, grad_input = lax.optimization_barrier((*far, hyena, grad_input))
    mine = added(row, *far)
    other = turn(mine, 0, 0, 1)
    conv_total, residue_total, skip_total = pl.pallas_call(
        spread_kernel,
        in_specs=[smem, vmem, vmem],
        out_shape=[
            struct((3, TAPS, channels), f32), struct((POLES, channels), f32),
            struct((1, channels), f32),
        ],
        compiler_params=roomy(16),
        name="spread",
    )(core[None].astype(jnp.int32), mine, other)
    return hyena, grad_input, conv_total, residue_total, skip_total[0]


def solution(mesh):
    in_specs = (
        P("seq"),
        P(None, "ch"),
        P("ch"),
        P(None, None, "ch"),
        P(None, "ch"),
        P(None, "ch"),
        P("ch"),
        P("seq", "ch"),
    )
    out_specs = (P("seq", "ch"), P("seq", "ch"), P(None, None, "ch"), P(None, "ch"), P("ch"))
    return jax.shard_map(
        per_device, mesh=mesh, in_specs=in_specs, out_specs=out_specs, check_vma=False
    )
```
